512 devices in a mesh: slab: 64 (over z, y_lo, core), sub: 8 (over x, y_hi).
Axes of the slice: x: 4, y: 8 (y_hi: 2, y_lo: 4; y = y_hi * 4 + y_lo), z: 8, core: 2. Of those that a mesh axis runs over, the one named last changes fastest.
Arguments:
- fields: float32 [3, 3, 3, 3, 128, 64, 128], P(None, None, None, None, 'slab', 'sub'), may hold values from 0.25 to 4
- speeds: float32 [3, 128, 64, 128], P(None, 'slab', 'sub'), may hold values from -4.5 to 4.5
Outputs:
- remapped: float32 [3, 3, 3, 3, 128, 64, 128], P(None, None, None, None, 'slab', 'sub')
The draws below stay inside these ranges and needn't reach their ends.
All inputs are finite; a program needn't handle non-finite values. Where the reference program divides by a largest or mean magnitude, that divisor is 1e-20 or more.
Results may differ from the reference program's by a relative error of at most 0.0001.
Values sent between devices are 32-bit elements; how exact they have to be, the bound alone decides.
A program may use at most 64 MiB of HBM per device.

```python
import math
import jax
import jax.numpy as jnp
from jax import lax

FIELDS = 3
NODES = 3
STEPS = 3
NX = 128
NY = 64
NZ = 128


def draw_speeds(key, part):
    key = jax.random.fold_in(key, 7)
    shape = (3, NX, NY, NZ)
    base = jnp.clip(jax.random.normal(key, shape, jnp.float32), -3.0, 3.0)
    ramp = 1.0 + 2.0 * (jnp.arange(NX, dtype=jnp.float32) + 0.5) / NX
    return 0.5 * base * ramp[None, :, None, None]


def level_of(rng, dims, pieces, low, top_value):
    factor_of = 1.0
    for axis_at, parts in pieces:
        steps = jax.random.uniform(jax.random.fold_in(jax.random.fold_in(rng, 6), axis_at), (parts,), jnp.float32, low / len(pieces), top_value / len(pieces))
        factor_of = factor_of * jnp.repeat(jnp.exp(steps), dims[axis_at] // parts).reshape((-1,) + (1,) * (len(dims) - 1 - axis_at))
    return factor_of


def setup_inputs(seed: int = 0) -> dict:
    key_list = jax.random.split(jax.random.key(seed), 3)
    return {
        "fields": jnp.clip(jnp.exp(math.log(4.0) - 2.7725887 * jax.random.uniform(key_list[0], (FIELDS, NODES, NODES, NODES, NX, NY, NZ), jnp.float32) ** level_of(key_list[0], (FIELDS, NODES, NODES, NODES, NX, NY, NZ), ((4, 64), (5, 8)), -0.2, 0.2)), 0.25, 4.0),
        "speeds": draw_speeds(jax.random.fold_in(key_list[2], 71), 0),
    }


DERIVATIVE = ((-1.5, 2.0, -0.5), (-0.5, 0.0, 0.5), (0.5, -2.0, 1.5))
QUAD_WEIGHTS = (1.0 / 3.0, 4.0 / 3.0, 1.0 / 3.0)
COURANT = 0.12
SOFTNESS = 0.05


def direction_term(values, interior, speed_lo, speed_hi, neighbour_low, neighbour_high, node_axis):
    node_slices = [lax.slice_in_dim(values, i, i + 1, axis=node_axis) for i in range(3)]
    face_low = node_slices[0]
    face_high = node_slices[2]
    flux_lo = jnp.maximum(speed_lo, 0.0) * neighbour_low + jnp.minimum(speed_lo, 0.0) * face_low
    flux_hi = jnp.maximum(speed_hi, 0.0) * face_high + jnp.minimum(speed_hi, 0.0) * neighbour_high
    outputs = []
    for i in range(3):
        gradient = DERIVATIVE[i][0] * node_slices[0] + DERIVATIVE[i][1] * node_slices[1] + DERIVATIVE[i][2] * node_slices[2]
        contrib = interior * gradient
        if i == 2:
            contrib = contrib + 3.0 * (flux_hi - interior * face_high)
        if i == 0:
            contrib = contrib - 3.0 * (flux_lo - interior * face_low)
        outputs.append(-2.0 * contrib)
    return jnp.concatenate(outputs, axis=node_axis)


def tendency(values, speed_lows, speed_highs, interiors):
    summed = None
    for d in range(3):
        node_axis = d
        element_axis = 3 + d
        face_low = lax.slice_in_dim(values, 0, 1, axis=node_axis)
        face_high = lax.slice_in_dim(values, 2, 3, axis=node_axis)
        neighbour_low = jnp.roll(face_high, 1, axis=element_axis)
        neighbour_high = jnp.roll(face_low, -1, axis=element_axis)
        contrib = direction_term(values, interiors[d], speed_lows[d], speed_highs[d], neighbour_low, neighbour_high, node_axis)
        summed = contrib if summed is None else summed + contrib
    return summed


def bounds(values):
    element_low = jnp.min(values, axis=(0, 1, 2))
    element_high = jnp.max(values, axis=(0, 1, 2))
    lowest = element_low
    highest = element_high
    for axis_index in range(3):
        for offset in (1, -1):
            lowest = jnp.minimum(lowest, jnp.roll(element_low, offset, axis=axis_index))
            highest = jnp.maximum(highest, jnp.roll(element_high, offset, axis=axis_index))
    return lowest, highest


def limiter(values, lowest, highest):
    weight_line = jnp.array(QUAD_WEIGHTS, dtype=values.dtype)
    weights = (weight_line[:, None, None] * weight_line[None, :, None] * weight_line[None, None, :] / 8.0)[:, :, :, None, None, None]
    average = jnp.sum(values * weights, axis=(0, 1, 2), keepdims=True)
    largest = jnp.max(values, axis=(0, 1, 2), keepdims=True)
    smallest = jnp.min(values, axis=(0, 1, 2), keepdims=True)
    upper_ratio = (jnp.maximum(highest[None, None, None] - average, 0.0) + SOFTNESS) / (largest - average + SOFTNESS)
    lower_ratio = (jnp.maximum(average - lowest[None, None, None], 0.0) + SOFTNESS) / (average - smallest + SOFTNESS)
    scaling = jnp.minimum(1.0, jnp.minimum(upper_ratio, lower_ratio))
    return average + scaling * (values - average)


def reference(fields, speeds):
    speed_lows = [speeds[d] for d in range(3)]
    speed_highs = [jnp.roll(speeds[d], -1, axis=d) for d in range(3)]
    interiors = [0.5 * (speed_lows[d] + speed_highs[d]) for d in range(3)]
    fastest = jnp.max(jnp.abs(interiors[0]) + jnp.abs(interiors[1]) + jnp.abs(interiors[2]))
    time_step = COURANT / (fastest + 1e-6)

    def evolve(current):
        for count in range(STEPS):
            lowest, highest = bounds(current)
            section_one = limiter(current + time_step * tendency(current, speed_lows, speed_highs, interiors), lowest, highest)
            section_two = limiter(0.75 * current + 0.25 * (section_one + time_step * tendency(section_one, speed_lows, speed_highs, interiors)), lowest, highest)
            current = limiter(current / 3.0 + (2.0 / 3.0) * (section_two + time_step * tendency(section_two, speed_lows, speed_highs, interiors)), lowest, highest)
        return current

    return lax.map(evolve, fields)
```

```python
import functools

import jax
import jax.numpy as jnp
from jax import lax
from jax.experimental import pallas as pl
from jax.experimental.pallas import tpu as pltpu
from jax.sharding import PartitionSpec as P

STEPS = 3
STAGES = 3 * STEPS
FIELDS = 3
ROWS = 2
COURANT = 0.12
SOFTNESS = 0.05
NODE_WEIGHTS = (1.0, 4.0, 1.0)
MESH = pl.DeviceIdType.MESH
X_TILES = 11
Y_ROWS = 24


def line_terms(v0, v1, v2, a, flux_lo, flux_hi):
    d = v2 - v0
    t = (v0 + v2) + 4.0 * v1
    big = a * t
    small = a * d
    twice = small + small
    return (big - twice) + flux_lo, small, -((big + twice) + flux_hi)


def kernel(
    n_slab,
    n_sub,
    fields_hbm,
    speeds_hbm,
    out_hbm,
    state,
    speeds,
    bounds,
    coef,
    send_x,
    recv_x,
    send_y,
    recv_y,
    speed_send,
    speed_recv_x,
    speed_recv_y,
    near_max,
    far_max,
    max_send,
    load_sem,
    store_sem,
    face_send_sem,
    face_recv_sem,
    speed_send_sem,
    speed_recv_sem,
    max_send_sem,
    max_recv_sem,
):
    slab = lax.axis_index("slab")
    sub = lax.axis_index("sub")
    n_near, n_far = near_max.shape[0], far_max.shape[0]
    near_at = lax.rem(sub, 2) * 8 + lax.rem(slab, 8)
    far_at = lax.div(slab, 8) * (n_sub // 2) + lax.div(sub, 2)

    def next_along(axis, by):
        size = {"slab": n_slab, "sub": n_sub}[axis]
        return {axis: lax.rem(lax.axis_index(axis) + (by + size), size)}

    def near_device(by):
        at = lax.rem(near_at + by, n_near)
        return {
            "slab": lax.div(slab, 8) * 8 + lax.rem(at, 8),
            "sub": lax.div(sub, 2) * 2 + lax.div(at, 8),
        }

    def far_device(by):
        at = lax.rem(far_at + by, n_far)
        return {
            "slab": lax.div(at, n_sub // 2) * 8 + lax.rem(slab, 8),
            "sub": lax.rem(at, n_sub // 2) * 2 + lax.rem(sub, 2),
        }

    load_speeds = pltpu.make_async_copy(speeds_hbm, speeds, load_sem.at[FIELDS])
    load_speeds.start()
    loads = []
    for f in range(FIELDS):
        load = pltpu.make_async_copy(fields_hbm.at[f], state.at[0, f], load_sem.at[f])
        load.start()
        loads.append(load)

    barrier = pltpu.get_barrier_semaphore()
    greeted = [next_along(axis, by) for axis in ("sub", "slab") for by in (1, -1)]
    greeted += [far_device(by) for by in range(1, n_far)]
    greeted += [near_device(by) for by in range(1, n_near)]
    for device in greeted:
        pl.semaphore_signal(barrier, inc=1, device_id=device, device_id_type=MESH)
    load_speeds.wait()
    for r in range(ROWS):
        speed_send[r : r + 1, :] = speeds[1, r, 0:1, :]
    pl.semaphore_wait(barrier, len(greeted))

    speed_y = pltpu.make_async_remote_copy(
        src_ref=speed_send,
        dst_ref=speed_recv_y,
        send_sem=speed_send_sem.at[0],
        recv_sem=speed_recv_sem.at[0],
        device_id=next_along("sub", -1),
        device_id_type=MESH,
    )
    speed_x = pltpu.make_async_remote_copy(
        src_ref=speeds.at[0, 0],
        dst_ref=speed_recv_x,
        send_sem=speed_send_sem.at[1],
        recv_sem=speed_recv_sem.at[1],
        device_id=next_along("slab", -1),
        device_id_type=MESH,
    )
    speed_y.start()
    speed_x.start()

    def face_copies(t, f):
        copies = []
        for axis, sent, received in (("sub", send_y, recv_y), ("slab", send_x, recv_x)):
            for way, by in ((0, 1), (1, -1)):
                at = (0 if axis == "sub" else 2) + way
                copies.append(
                    pltpu.make_async_remote_copy(
                        src_ref=sent.at[t, f, way],
                        dst_ref=received.at[t, f, way],
                        send_sem=face_send_sem.at[t, f, at],
                        recv_sem=face_recv_sem.at[t, f, at],
                        device_id=next_along(axis, by),
                        device_id_type=MESH,
                    )
                )
        return copies

    def pack_faces(t, f, r, values):
        for i in range(3):
            for j in range(3):
                for k in range(3):
                    v = values[i][j][k]
                    if i == 2 and r == ROWS - 1:
                        send_x[t, f, 0, 3 * j + k] = v
                    if i == 0 and r == 0:
                        send_x[t, f, 1, 3 * j + k] = v
                    at = 9 * r + 3 * i + k
                    if j == 2:
                        send_y[t, f, 0, at : at + 1, :] = v[7:8, :]
                    if j == 0:
                        send_y[t, f, 1, at : at + 1, :] = v[0:1, :]

    def pack_bounds(t, f, r, lowest, highest):
        for n, v in ((0, lowest), (1, highest)):
            bounds[f, r, n] = v
            if r == ROWS - 1:
                send_x[t, f, 0, 9 + n] = v
            if r == 0:
                send_x[t, f, 1, 9 + n] = v
            at = 18 + 2 * r + n
            send_y[t, f, 0, at : at + 1, :] = v[7:8, :]
            send_y[t, f, 1, at : at + 1, :] = v[0:1, :]

    def first_faces(f, _):
        for r in range(ROWS):
            values = [
                [[state[0, f, i, j, k, r] for k in range(3)] for j in range(3)] for i in range(3)
            ]
            flat = [values[i][j][k] for i in range(3) for j in range(3) for k in range(3)]
            pack_faces(0, f, r, values)
            pack_bounds(
                0, f, r, functools.reduce(jnp.minimum, flat), functools.reduce(jnp.maximum, flat)
            )
        for copy in face_copies(0, f):
            copy.start()
        return 0

    for load in loads:
        load.wait()
    lax.fori_loop(0, FIELDS, first_faces, 0)

    row_at = lax.broadcasted_iota(jnp.int32, (8, 128), 0)
    at_bottom = row_at == 0
    at_top = row_at == 7

    speed_y.wait_recv()
    speed_x.wait_recv()
    face_x = [speeds[0, r] for r in range(ROWS)] + [speed_recv_x[...]]
    y_lo = [speeds[1, r] for r in range(ROWS)]
    y_hi = [
        jnp.where(
            at_top,
            jnp.broadcast_to(speed_recv_y[r : r + 1, :], (8, 128)),
            pltpu.roll(y_lo[r], 7, 0),
        )
        for r in range(ROWS)
    ]
    z_lo = [speeds[2, r] for r in range(ROWS)]
    interiors = [
        [0.5 * (face_x[r] + face_x[r + 1]) for r in range(ROWS)],
        [0.5 * (y_lo[r] + y_hi[r]) for r in range(ROWS)],
        [0.5 * (z_lo[r] + pltpu.roll(z_lo[r], 127, 1)) for r in range(ROWS)],
    ]
    fast = None
    for r in range(ROWS):
        total = jnp.abs(interiors[0][r]) + jnp.abs(interiors[1][r]) + jnp.abs(interiors[2][r])
        fast = total if fast is None else jnp.maximum(fast, total)
    fast = jnp.max(fast, axis=0, keepdims=True)
    max_copies = []
    for phase, (received, device_of) in enumerate(((near_max, near_device), (far_max, far_device))):
        n = received.shape[0]
        received[0] = fast
        if n > 1:
            max_send[phase] = fast
            for by in range(1, n):
                copy = pltpu.make_async_remote_copy(
                    src_ref=max_send.at[phase],
                    dst_ref=received.at[by],
                    send_sem=max_send_sem.at[phase],
                    recv_sem=max_recv_sem.at[phase],
                    device_id=device_of(by),
                    device_id_type=MESH,
                )
                copy.start()
            pltpu.make_async_copy(
                received.at[pl.ds(1, n - 1)], received.at[pl.ds(1, n - 1)], max_recv_sem.at[phase]
            ).wait()
            fast = jnp.max(received[...], axis=0)
    fastest = jnp.max(jnp.broadcast_to(fast, (8, 128)), axis=1, keepdims=True)
    time_step = COURANT / (jnp.broadcast_to(fastest, (8, 128)) + 1e-6)
    six = 6.0 * time_step
    up = lambda s: six * jnp.maximum(s, 0.0)
    down = lambda s: six * jnp.minimum(s, 0.0)
    for r in range(ROWS):
        for d in range(3):
            coef[3 * r + d] = -(time_step * interiors[d][r])
        for n, v in enumerate(
            (up(y_lo[r]), down(y_lo[r]), up(y_hi[r]), down(y_hi[r]), up(z_lo[r]), down(z_lo[r]))
        ):
            coef[6 + 6 * r + n] = v
    for q in range(ROWS + 1):
        coef[18 + 2 * q] = up(face_x[q])
        coef[19 + 2 * q] = down(face_x[q])

    def stage(n, _):
        t = lax.div(n, FIELDS)
        f = lax.rem(n, FIELDS)
        part = lax.rem(t, 3)
        source = part
        target = lax.rem(part + 1, 3)
        share = jnp.where(part == 0, 0.0, jnp.where(part == 1, 0.75, 1.0 / 3.0)).astype(jnp.float32)
        rest = jnp.where(part == 0, 1.0, jnp.where(part == 1, 0.25, 2.0 / 3.0)).astype(jnp.float32)
        for copy in face_copies(t, f):
            copy.wait_recv()

        @pl.when(part == 0)
        def _():
            low = [bounds[f, r, 0] for r in range(ROWS)]
            high = [bounds[f, r, 1] for r in range(ROWS)]
            for values, at, pick in ((low, 0, jnp.minimum), (high, 1, jnp.maximum)):
                ring = [recv_x[t, f, 0, 9 + at]] + values + [recv_x[t, f, 1, 9 + at]]
                for r in range(ROWS):
                    here = 18 + 2 * r + at
                    v = values[r]
                    below = jnp.where(
                        at_bottom,
                        jnp.broadcast_to(recv_y[t, f, 0, here : here + 1, :], (8, 128)),
                        pltpu.roll(v, 1, 0),
                    )
                    above = jnp.where(
                        at_top,
                        jnp.broadcast_to(recv_y[t, f, 1, here : here + 1, :], (8, 128)),
                        pltpu.roll(v, 7, 0),
                    )
                    best = pick(pick(v, ring[r]), ring[r + 2])
                    best = pick(best, pick(below, above))
                    best = pick(best, pick(pltpu.roll(v, 1, 1), pltpu.roll(v, 127, 1)))
                    bounds[f, r, 2 + at] = best

        for r in range(ROWS):
            v = [
                [[state[source, f, i, j, k, r] for k in range(3)] for j in range(3)]
                for i in range(3)
            ]
            new = [[[v[i][j][k] for k in range(3)] for j in range(3)] for i in range(3)]
            a = [coef[3 * r + d] for d in range(3)]
            up_x = [coef[18 + 2 * q] for q in (r, r + 1)]
            down_x = [coef[19 + 2 * q] for q in (r, r + 1)]
            up_y, down_y, up_y_hi, down_y_hi, up_z, down_z = [coef[6 + 6 * r + n] for n in range(6)]
            for k in range(3):
                for j in range(3):
                    at = 3 * j + k
                    if r == 0:
                        before = recv_x[t, f, 0, at]
                    else:
                        before = state[source, f, 2, j, k, r - 1]
                    if r == ROWS - 1:
                        after = recv_x[t, f, 1, at]
                    else:
                        after = state[source, f, 0, j, k, r + 1]
                    flux_lo = up_x[0] * before + down_x[0] * v[0][j][k]
                    flux_hi = up_x[1] * v[2][j][k] + down_x[1] * after
                    terms = line_terms(v[0][j][k], v[1][j][k], v[2][j][k], a[0], flux_lo, flux_hi)
                    for i in range(3):
                        new[i][j][k] = new[i][j][k] + terms[i]
                for i in range(3):
                    at = 9 * r + 3 * i + k
                    before = jnp.where(
                        at_bottom,
                        jnp.broadcast_to(recv_y[t, f, 0, at : at + 1, :], (8, 128)),
                        pltpu.roll(v[i][2][k], 1, 0),
                    )
                    after = jnp.where(
                        at_top,
                        jnp.broadcast_to(recv_y[t, f, 1, at : at + 1, :], (8, 128)),
                        pltpu.roll(v[i][0][k], 7, 0),
                    )
                    flux_lo = up_y * before + down_y * v[i][0][k]
                    flux_hi = up_y_hi * v[i][2][k] + down_y_hi * after
                    terms = line_terms(v[i][0][k], v[i][1][k], v[i][2][k], a[1], flux_lo, flux_hi)
                    for j in range(3):
                        new[i][j][k] = new[i][j][k] + terms[j]
            average = largest = smallest = None
            for i in range(3):
                for j in range(3):
                    flux_lo = up_z * pltpu.roll(v[i][j][2], 1, 1) + down_z * v[i][j][0]
                    flux_hi = pltpu.roll(flux_lo, 127, 1)
                    terms = line_terms(v[i][j][0], v[i][j][1], v[i][j][2], a[2], flux_lo, flux_hi)
                    for k in range(3):
                        x = share * state[0, f, i, j, k, r] + rest * (new[i][j][k] + terms[k])
                        new[i][j][k] = x
                        largest = x if largest is None else jnp.maximum(largest, x)
                        smallest = x if smallest is None else jnp.minimum(smallest, x)
                    line = (new[i][j][0] + new[i][j][2]) + 4.0 * new[i][j][1]
                    weight = NODE_WEIGHTS[i] * NODE_WEIGHTS[j]
                    line = line if weight == 1.0 else weight * line
                    average = line if average is None else average + line
            average = average * (1.0 / 216.0)
            lowest = bounds[f, r, 2]
            highest = bounds[f, r, 3]
            upper = (jnp.maximum(highest - average, 0.0) + SOFTNESS) / (largest - average + SOFTNESS)
            lower = (jnp.maximum(average - lowest, 0.0) + SOFTNESS) / (average - smallest + SOFTNESS)
            scaling = jnp.minimum(1.0, jnp.minimum(upper, lower))
            offset = average - scaling * average
            for i in range(3):
                for j in range(3):
                    for k in range(3):
                        x = scaling * new[i][j][k] + offset
                        new[i][j][k] = x
                        state[target, f, i, j, k, r] = x

            @pl.when(t < STAGES - 1)
            def _():
                pack_faces(t + 1, f, r, new)
                pack_bounds(t + 1, f, r, scaling * smallest + offset, scaling * largest + offset)

        @pl.when(t < STAGES - 1)
        def _():
            for copy in face_copies(t + 1, f):
                copy.start()

        @pl.when(t == STAGES - 1)
        def _():
            pltpu.make_async_copy(state.at[0, f], out_hbm.at[f], store_sem.at[f]).start()

        return 0

    lax.fori_loop(0, STAGES * FIELDS, stage, 0)

    speed_y.wait_send()
    speed_x.wait_send()
    for phase, received in enumerate((near_max, far_max)):
        n = received.shape[0]
        if n > 1:
            pltpu.make_async_copy(
                received.at[pl.ds(1, n - 1)], received.at[pl.ds(1, n - 1)], max_send_sem.at[phase]
            ).wait()

    def drain(n, _):
        for copy in face_copies(lax.div(n, FIELDS), lax.rem(n, FIELDS)):
            copy.wait_send()
        return 0

    lax.fori_loop(0, STAGES * FIELDS, drain, 0)
    for f in range(FIELDS):
        pltpu.make_async_copy(state.at[0, f], out_hbm.at[f], store_sem.at[f]).wait()


def solution(mesh):
    n_slab, n_sub = mesh.shape["slab"], mesh.shape["sub"]
    n_near = 16
    n_far = n_slab * n_sub // n_near

    def on_device(fields, speeds):
        vmem = lambda *shape: pltpu.VMEM(shape, jnp.float32)
        dma = lambda *shape: pltpu.SemaphoreType.DMA(shape)
        return pl.pallas_call(
            functools.partial(kernel, n_slab, n_sub),
            out_shape=jax.ShapeDtypeStruct(fields.shape, fields.dtype),
            in_specs=[pl.BlockSpec(memory_space=pl.ANY)] * 2,
            out_specs=pl.BlockSpec(memory_space=pl.ANY),
            scratch_shapes=[
                vmem(3, FIELDS, 3, 3, 3, ROWS, 8, 128),
                vmem(3, ROWS, 8, 128),
                vmem(FIELDS, ROWS, 4, 8, 128),
                vmem(24, 8, 128),
                vmem(STAGES, FIELDS, 2, X_TILES, 8, 128),
                vmem(STAGES, FIELDS, 2, X_TILES, 8, 128),
                vmem(STAGES, FIELDS, 2, Y_ROWS, 128),
                vmem(STAGES, FIELDS, 2, Y_ROWS, 128),
                vmem(8, 128),
                vmem(8, 128),
                vmem(8, 128),
                vmem(n_near, 1, 128),
                vmem(n_far, 1, 128),
                vmem(2, 1, 128),
                dma(FIELDS + 1),
                dma(FIELDS),
                dma(STAGES, FIELDS, 4),
                dma(STAGES, FIELDS, 4),
                dma(2),
                dma(2),
                dma(2),
                dma(2),
            ],
            compiler_params=pltpu.CompilerParams(
                collective_id=1, has_side_effects=True, vmem_limit_bytes=48 * 1024 * 1024
            ),
            name="remap",
        )(fields, speeds)

    spec = P(None, None, None, None, "slab", "sub", None)
    return jax.shard_map(
        on_device,
        mesh=mesh,
        in_specs=(spec, P(None, "slab", "sub", None)),
        out_specs=spec,
        check_vma=False,
    )
```

```python
import functools

import jax
import jax.numpy as jnp
from jax import lax
from jax.experimental import pallas as pl
from jax.experimental.pallas import tpu as pltpu
from jax.sharding import PartitionSpec as P

STEPS = 3
STAGES = 3 * STEPS
FIELDS = 3
ROWS = 2
COURANT = 0.12
SOFTNESS = 0.05
NODE_WEIGHTS = (1.0, 4.0, 1.0)
MESH = pl.DeviceIdType.MESH
X_TILES, X_NODES = 11, 9
Y_ROWS, Y_USED, Y_NODES = 24, 22, 18


def tree(pick, values):
    while len(values) > 1:
        values = [
            pick(values[n], values[n + 1]) if n + 1 < len(values) else values[n]
            for n in range(0, len(values), 2)
        ]
    return values[0]


def line_terms(v0, v1, v2, a, flux_lo, flux_hi):
    d = v2 - v0
    t = (v0 + v2) + 4.0 * v1
    big = a * t
    small = a * d
    twice = small + small
    return (big - twice) + flux_lo, small, -((big + twice) + flux_hi)


def kernel(
    n_slab,
    n_sub,
    fields_hbm,
    speeds_hbm,
    out_hbm,
    state,
    partial,
    speeds,
    bounds,
    coef,
    send_x,
    recv_x,
    send_y,
    recv_y,
    speed_send,
    speed_recv_x,
    speed_recv_y,
    near_max,
    far_max,
    max_send,
    load_sem,
    store_sem,
    face_send_sem,
    face_recv_sem,
    speed_send_sem,
    speed_recv_sem,
    max_send_sem,
    max_recv_sem,
):
    slab = lax.axis_index("slab")
    sub = lax.axis_index("sub")
    n_near, n_far = near_max.shape[0], far_max.shape[0]
    near_at = lax.rem(sub, 2) * 8 + lax.rem(slab, 8)
    far_at = lax.div(slab, 8) * (n_sub // 2) + lax.div(sub, 2)

    def next_along(axis, by):
        size = {"slab": n_slab, "sub": n_sub}[axis]
        return {axis: lax.rem(lax.axis_index(axis) + (by + size), size)}

    def near_device(by):
        at = lax.rem(near_at + by, n_near)
        return {
            "slab": lax.div(slab, 8) * 8 + lax.rem(at, 8),
            "sub": lax.div(sub, 2) * 2 + lax.div(at, 8),
        }

    def far_device(by):
        at = lax.rem(far_at + by, n_far)
        return {
            "slab": lax.div(at, n_sub // 2) * 8 + lax.rem(slab, 8),
            "sub": lax.rem(at, n_sub // 2) * 2 + lax.rem(sub, 2),
        }

    load_speeds = pltpu.make_async_copy(speeds_hbm, speeds, load_sem.at[FIELDS])
    load_speeds.start()
    loads = []
    for f in range(FIELDS):
        load = pltpu.make_async_copy(fields_hbm.at[f], state.at[0, f], load_sem.at[f])
        load.start()
        loads.append(load)

    barrier = pltpu.get_barrier_semaphore()
    greeted = [next_along(axis, by) for axis in ("sub", "slab") for by in (1, -1)]
    greeted += [far_device(by) for by in range(1, n_far)]
    greeted += [near_device(by) for by in range(1, n_near)]
    for device in greeted:
        pl.semaphore_signal(barrier, inc=1, device_id=device, device_id_type=MESH)
    load_speeds.wait()
    for r in range(ROWS):
        speed_send[r : r + 1, :] = speeds[1, r, 0:1, :]
    pl.semaphore_wait(barrier, len(greeted))

    speed_y = pltpu.make_async_remote_copy(
        src_ref=speed_send,
        dst_ref=speed_recv_y,
        send_sem=speed_send_sem.at[0],
        recv_sem=speed_recv_sem.at[0],
        device_id=next_along("sub", -1),
        device_id_type=MESH,
    )
    speed_x = pltpu.make_async_remote_copy(
        src_ref=speeds.at[0, 0],
        dst_ref=speed_recv_x,
        send_sem=speed_send_sem.at[1],
        recv_sem=speed_recv_sem.at[1],
        device_id=next_along("slab", -1),
        device_id_type=MESH,
    )
    speed_y.start()
    speed_x.start()

    def face_copies(t, f, with_bounds):
        copies = []
        for axis, sent, received, size in (
            ("sub", send_y, recv_y, Y_USED if with_bounds else Y_NODES),
            ("slab", send_x, recv_x, X_TILES if with_bounds else X_NODES),
        ):
            for way, by in ((0, 1), (1, -1)):
                at = (0 if axis == "sub" else 2) + way
                copies.append(
                    pltpu.make_async_remote_copy(
                        src_ref=sent.at[t, f, way, pl.ds(0, size)],
                        dst_ref=received.at[t, f, way, pl.ds(0, size)],
                        send_sem=face_send_sem.at[t, f, at],
                        recv_sem=face_recv_sem.at[t, f, at],
                        device_id=next_along(axis, by),
                        device_id_type=MESH,
                    )
                )
        return copies

    def for_faces(t, f, action):
        @pl.when(lax.rem(t, 3) == 0)
        def _():
            for copy in face_copies(t, f, True):
                action(copy)

        @pl.when(lax.rem(t, 3) != 0)
        def _():
            for copy in face_copies(t, f, False):
                action(copy)

    def pack_faces(t, f, r, values):
        for i in range(3):
            for j in range(3):
                for k in range(3):
                    v = values[i][j][k]
                    if i == 2 and r == ROWS - 1:
                        send_x[t, f, 0, 3 * j + k] = v
                    if i == 0 and r == 0:
                        send_x[t, f, 1, 3 * j + k] = v
                    at = 9 * r + 3 * i + k
                    if j == 2:
                        send_y[t, f, 0, at : at + 1, :] = v[7:8, :]
                    if j == 0:
                        send_y[t, f, 1, at : at + 1, :] = v[0:1, :]

    def pack_bounds(t, f, r, lowest, highest):
        for n, v in ((0, lowest), (1, highest)):
            bounds[f, r, n] = v
            if r == ROWS - 1:
                send_x[t, f, 0, 9 + n] = v
            if r == 0:
                send_x[t, f, 1, 9 + n] = v
            at = 18 + 2 * r + n
            send_y[t, f, 0, at : at + 1, :] = v[7:8, :]
            send_y[t, f, 1, at : at + 1, :] = v[0:1, :]

    def first_faces(f, _):
        for r in range(ROWS):
            values = [
                [[state[0, f, i, j, k, r] for k in range(3)] for j in range(3)] for i in range(3)
            ]
            flat = [values[i][j][k] for i in range(3) for j in range(3) for k in range(3)]
            pack_faces(0, f, r, values)
            pack_bounds(
                0, f, r, tree(jnp.minimum, flat), tree(jnp.maximum, flat)
            )
        for copy in face_copies(0, f, True):
            copy.start()
        return 0

    for load in loads:
        load.wait()
    lax.fori_loop(0, FIELDS, first_faces, 0)

    row_at = lax.broadcasted_iota(jnp.int32, (8, 128), 0)
    at_bottom = row_at == 0
    at_top = row_at == 7

    speed_y.wait_recv()
    speed_x.wait_recv()
    face_x = [speeds[0, r] for r in range(ROWS)] + [speed_recv_x[...]]
    y_lo = [speeds[1, r] for r in range(ROWS)]
    y_hi = [
        jnp.where(
            at_top,
            jnp.broadcast_to(speed_recv_y[r : r + 1, :], (8, 128)),
            pltpu.roll(y_lo[r], 7, 0),
        )
        for r in range(ROWS)
    ]
    z_lo = [speeds[2, r] for r in range(ROWS)]
    interiors = [
        [0.5 * (face_x[r] + face_x[r + 1]) for r in range(ROWS)],
        [0.5 * (y_lo[r] + y_hi[r]) for r in range(ROWS)],
        [0.5 * (z_lo[r] + pltpu.roll(z_lo[r], 127, 1)) for r in range(ROWS)],
    ]
    fast = None
    for r in range(ROWS):
        total = jnp.abs(interiors[0][r]) + jnp.abs(interiors[1][r]) + jnp.abs(interiors[2][r])
        fast = total if fast is None else jnp.maximum(fast, total)
    fast = jnp.max(fast, axis=0, keepdims=True)
    max_copies = []
    for phase, (received, device_of) in enumerate(((near_max, near_device), (far_max, far_device))):
        n = received.shape[0]
        received[0] = fast
        if n > 1:
            max_send[phase] = fast
            for by in range(1, n):
                copy = pltpu.make_async_remote_copy(
                    src_ref=max_send.at[phase],
                    dst_ref=received.at[by],
                    send_sem=max_send_sem.at[phase],
                    recv_sem=max_recv_sem.at[phase],
                    device_id=device_of(by),
                    device_id_type=MESH,
                )
                copy.start()
            pltpu.make_async_copy(
                received.at[pl.ds(1, n - 1)], received.at[pl.ds(1, n - 1)], max_recv_sem.at[phase]
            ).wait()
            fast = jnp.max(received[...], axis=0)
    fastest = jnp.max(jnp.broadcast_to(fast, (8, 128)), axis=1, keepdims=True)
    time_step = COURANT / (jnp.broadcast_to(fastest, (8, 128)) + 1e-6)
    six = 6.0 * time_step
    up = lambda s: six * jnp.maximum(s, 0.0)
    down = lambda s: six * jnp.minimum(s, 0.0)
    for r in range(ROWS):
        for d in range(3):
            coef[3 * r + d] = -(time_step * interiors[d][r])
        y_up, y_down = up(y_lo[r]), down(y_hi[r])
        for n, v in enumerate(
            (
                jnp.where(at_bottom, 0.0, y_up),
                down(y_lo[r]),
                up(y_hi[r]),
                jnp.where(at_top, 0.0, y_down),
                up(z_lo[r]),
                down(z_lo[r]),
                jnp.where(at_bottom, y_up, 0.0),
                jnp.where(at_top, y_down, 0.0),
            )
        ):
            coef[6 + 8 * r + n] = v
    for q in range(ROWS + 1):
        coef[22 + 2 * q] = up(face_x[q])
        coef[23 + 2 * q] = down(face_x[q])

    def shares(t):
        part = lax.rem(t, 3)
        pick = lambda *values: jnp.where(
            part == 0, values[0], jnp.where(part == 1, values[1], values[2])
        ).astype(jnp.float32)
        return pick(0.0, 0.75, 1.0 / 3.0), pick(1.0, 0.25, 2.0 / 3.0)

    def inner_part(t, f):
        source = lax.rem(t, 3)
        share, rest = shares(t)
        for r in range(ROWS):
            v = [
                [[state[source, f, i, j, k, r] for k in range(3)] for j in range(3)]
                for i in range(3)
            ]
            new = [[[v[i][j][k] for k in range(3)] for j in range(3)] for i in range(3)]
            a = [coef[3 * r + d] for d in range(3)]
            up_x = [coef[22 + 2 * q] for q in (r, r + 1)]
            down_x = [coef[23 + 2 * q] for q in (r, r + 1)]
            up_y, down_y, up_y_hi, down_y_hi, up_z, down_z = [coef[6 + 8 * r + n] for n in range(6)]
            for k in range(3):
                for j in range(3):
                    flux_lo = down_x[0] * v[0][j][k]
                    if r > 0:
                        flux_lo = flux_lo + up_x[0] * state[source, f, 2, j, k, r - 1]
                    flux_hi = up_x[1] * v[2][j][k]
                    if r < ROWS - 1:
                        flux_hi = flux_hi + down_x[1] * state[source, f, 0, j, k, r + 1]
                    terms = line_terms(v[0][j][k], v[1][j][k], v[2][j][k], a[0], flux_lo, flux_hi)
                    for i in range(3):
                        new[i][j][k] = new[i][j][k] + terms[i]
                for i in range(3):
                    flux_lo = up_y * pltpu.roll(v[i][2][k], 1, 0) + down_y * v[i][0][k]
                    flux_hi = up_y_hi * v[i][2][k] + down_y_hi * pltpu.roll(v[i][0][k], 7, 0)
                    terms = line_terms(v[i][0][k], v[i][1][k], v[i][2][k], a[1], flux_lo, flux_hi)
                    for j in range(3):
                        new[i][j][k] = new[i][j][k] + terms[j]
            for i in range(3):
                for j in range(3):
                    flux_lo = up_z * pltpu.roll(v[i][j][2], 1, 1) + down_z * v[i][j][0]
                    flux_hi = pltpu.roll(flux_lo, 127, 1)
                    terms = line_terms(v[i][j][0], v[i][j][1], v[i][j][2], a[2], flux_lo, flux_hi)
                    for k in range(3):
                        partial[f, i, j, k, r] = share * state[0, f, i, j, k, r] + rest * (
                            new[i][j][k] + terms[k]
                        )

    def spread(row):
        return jnp.broadcast_to(row, (8, 128))

    def gather_bounds(t, f):
        for at, pick in ((0, jnp.minimum), (1, jnp.maximum)):
            values = [bounds[f, r, at] for r in range(ROWS)]
            ring = [recv_x[t, f, 0, 9 + at]] + values + [recv_x[t, f, 1, 9 + at]]
            for r in range(ROWS):
                here = 18 + 2 * r + at
                v = values[r]
                below = jnp.where(
                    at_bottom, spread(recv_y[t, f, 0, here : here + 1, :]), pltpu.roll(v, 1, 0)
                )
                above = jnp.where(
                    at_top, spread(recv_y[t, f, 1, here : here + 1, :]), pltpu.roll(v, 7, 0)
                )
                best = pick(pick(v, ring[r]), ring[r + 2])
                best = pick(best, pick(below, above))
                best = pick(best, pick(pltpu.roll(v, 1, 1), pltpu.roll(v, 127, 1)))
                bounds[f, r, 2 + at] = best

    def outer_part(t, f):
        target = lax.rem(t + 1, 3)
        _, rest = shares(t)
        for r in range(ROWS):
            x = [
                [[partial[f, i, j, k, r] for k in range(3)] for j in range(3)] for i in range(3)
            ]
            up_y, down_y = [rest * coef[12 + 8 * r + n] for n in range(2)]
            for k in range(3):
                for j in range(3):
                    if r == 0:
                        up_x = rest * coef[22]
                        x[0][j][k] = x[0][j][k] + up_x * recv_x[t, f, 0, 3 * j + k]
                    if r == ROWS - 1:
                        down_x = rest * coef[23 + 2 * ROWS]
                        x[2][j][k] = x[2][j][k] - down_x * recv_x[t, f, 1, 3 * j + k]
                for i in range(3):
                    at = 9 * r + 3 * i + k
                    x[i][0][k] = x[i][0][k] + up_y * spread(recv_y[t, f, 0, at : at + 1, :])
                    x[i][2][k] = x[i][2][k] - down_y * spread(recv_y[t, f, 1, at : at + 1, :])
            averages, tops, bottoms = [], [], []
            for i in range(3):
                for j in range(3):
                    lo, mid, hi = x[i][j]
                    tops.append(jnp.maximum(jnp.maximum(lo, hi), mid))
                    bottoms.append(jnp.minimum(jnp.minimum(lo, hi), mid))
                    line = (lo + hi) + 4.0 * mid
                    weight = NODE_WEIGHTS[i] * NODE_WEIGHTS[j]
                    averages.append(line if weight == 1.0 else weight * line)
            average = tree(jnp.add, averages) * (1.0 / 216.0)
            largest = tree(jnp.maximum, tops)
            smallest = tree(jnp.minimum, bottoms)
            lowest = bounds[f, r, 2]
            highest = bounds[f, r, 3]
            upper = (jnp.maximum(highest - average, 0.0) + SOFTNESS) / (largest - average + SOFTNESS)
            lower = (jnp.maximum(average - lowest, 0.0) + SOFTNESS) / (average - smallest + SOFTNESS)
            scaling = jnp.minimum(1.0, jnp.minimum(upper, lower))
            offset = average - scaling * average
            for i in range(3):
                for j in range(3):
                    for k in range(3):
                        x[i][j][k] = scaling * x[i][j][k] + offset
                        state[target, f, i, j, k, r] = x[i][j][k]
            pack_faces(t + 1, f, r, x)
            pack_bounds(t + 1, f, r, scaling * smallest + offset, scaling * largest + offset)

    def stage(n, _):
        t = lax.div(n, FIELDS)
        f = lax.rem(n, FIELDS)

        @pl.when(t == 0)
        def _():
            inner_part(0, f)

        for_faces(t, f, lambda copy: copy.wait_recv())

        @pl.when(lax.rem(t, 3) == 0)
        def _():
            gather_bounds(t, f)

        outer_part(t, f)

        @pl.when(t < STAGES - 1)
        def _():
            for_faces(t + 1, f, lambda copy: copy.start())
            inner_part(t + 1, f)

        @pl.when(t == STAGES - 1)
        def _():
            pltpu.make_async_copy(state.at[0, f], out_hbm.at[f], store_sem.at[f]).start()

        return 0

    lax.fori_loop(0, STAGES * FIELDS, stage, 0)

    speed_y.wait_send()
    speed_x.wait_send()
    for phase, received in enumerate((near_max, far_max)):
        n = received.shape[0]
        if n > 1:
            pltpu.make_async_copy(
                received.at[pl.ds(1, n - 1)], received.at[pl.ds(1, n - 1)], max_send_sem.at[phase]
            ).wait()

    def drain(n, _):
        for_faces(lax.div(n, FIELDS), lax.rem(n, FIELDS), lambda copy: copy.wait_send())
        return 0

    lax.fori_loop(0, STAGES * FIELDS, drain, 0)
    for f in range(FIELDS):
        pltpu.make_async_copy(state.at[0, f], out_hbm.at[f], store_sem.at[f]).wait()


def solution(mesh):
    n_slab, n_sub = mesh.shape["slab"], mesh.shape["sub"]
    n_near = 16
    n_far = n_slab * n_sub // n_near

    def on_device(fields, speeds):
        vmem = lambda *shape: pltpu.VMEM(shape, jnp.float32)
        dma = lambda *shape: pltpu.SemaphoreType.DMA(shape)
        return pl.pallas_call(
            functools.partial(kernel, n_slab, n_sub),
            out_shape=jax.ShapeDtypeStruct(fields.shape, fields.dtype),
            in_specs=[pl.BlockSpec(memory_space=pltpu.HBM)] * 2,
            out_specs=pl.BlockSpec(memory_space=pl.ANY),
            scratch_shapes=[
                vmem(3, FIELDS, 3, 3, 3, ROWS, 8, 128),
                vmem(FIELDS, 3, 3, 3, ROWS, 8, 128),
                vmem(3, ROWS, 8, 128),
                vmem(FIELDS, ROWS, 4, 8, 128),
                vmem(24 + 2 * ROWS, 8, 128),
                vmem(STAGES + 1, FIELDS, 2, X_TILES, 8, 128),
                vmem(STAGES, FIELDS, 2, X_TILES, 8, 128),
                vmem(STAGES + 1, FIELDS, 2, Y_ROWS, 128),
                vmem(STAGES, FIELDS, 2, Y_ROWS, 128),
                vmem(8, 128),
                vmem(8, 128),
                vmem(8, 128),
                vmem(n_near, 1, 128),
                vmem(n_far, 1, 128),
                vmem(2, 1, 128),
                dma(FIELDS + 1),
                dma(FIELDS),
                dma(STAGES, FIELDS, 4),
                dma(STAGES, FIELDS, 4),
                dma(2),
                dma(2),
                dma(2),
                dma(2),
            ],
            compiler_params=pltpu.CompilerParams(
                collective_id=1, has_side_effects=True, vmem_limit_bytes=60 * 1024 * 1024
            ),
            name="remap",
        )(fields, speeds)

    spec = P(None, None, None, None, "slab", "sub", None)
    return jax.shard_map(
        on_device,
        mesh=mesh,
        in_specs=(spec, P(None, "slab", "sub", None)),
        out_specs=spec,
        check_vma=False,
    )
```

```python
import functools

import jax
import jax.numpy as jnp
from jax import lax
from jax.experimental import pallas as pl
from jax.experimental.pallas import tpu as pltpu
from jax.sharding import PartitionSpec as P

STEPS = 3
STAGES = 3 * STEPS
FIELDS = 3
ROWS = 2
COURANT = 0.12
SOFTNESS = 0.05
NODE_WEIGHTS = (1.0, 4.0, 1.0)
MESH = pl.DeviceIdType.MESH
X_TILES, X_NODES = 11, 9
Y_ROWS, Y_USED, Y_NODES = 24, 22, 18


def ring_distance(by, size):
    return min(by, size - by)


def farthest_first(outer, inner, hops):
    steps = [(a, b) for a in range(outer) for b in range(inner) if a or b]
    return sorted(steps, key=lambda step: -hops(*step))


def tree(pick, values):
    while len(values) > 1:
        values = [
            pick(values[n], values[n + 1]) if n + 1 < len(values) else values[n]
            for n in range(0, len(values), 2)
        ]
    return values[0]


def line_terms(v0, v1, v2, a, flux_lo, flux_hi):
    d = v2 - v0
    t = (v0 + v2) + 4.0 * v1
    big = a * t
    small = a * d
    twice = small + small
    return (big - twice) + flux_lo, small, -((big + twice) + flux_hi)


def kernel(
    n_slab,
    n_sub,
    fields_hbm,
    speeds_hbm,
    out_hbm,
    state,
    partial,
    speeds,
    bounds,
    coef,
    send_x,
    recv_x,
    send_y,
    recv_y,
    speed_send,
    speed_recv_x,
    speed_recv_y,
    near_max,
    far_max,
    max_send,
    load_sem,
    store_sem,
    face_send_sem,
    face_recv_sem,
    speed_send_sem,
    speed_recv_sem,
    max_send_sem,
    max_recv_sem,
):
    slab = lax.axis_index("slab")
    sub = lax.axis_index("sub")
    n_z, n_x = n_slab // 8, n_sub // 2

    def shifted(at, by, size):
        moved = at + by
        return jnp.where(moved >= size, moved - size, moved)

    z, l = lax.div(slab, 8), lax.rem(slab, 8)
    x, h = lax.div(sub, 2), lax.rem(sub, 2)
    along_l = [8 * z + shifted(l, by, 8) for by in range(8)]
    along_h = [2 * x + shifted(h, by, 2) for by in range(2)]
    along_z = [8 * shifted(z, by, n_z) + l for by in range(n_z)]
    along_x = [2 * shifted(x, by, n_x) + h for by in range(n_x)]
    near = [
        (2 * by_l + by_h, {"slab": along_l[by_l], "sub": along_h[by_h]})
        for by_h, by_l in farthest_first(
            2, 8, lambda by_h, by_l: ring_distance((4 * by_h + by_l // 2) % 8, 8)
        )
    ]
    far = [
        (n_x * by_z + by_x, {"slab": along_z[by_z], "sub": along_x[by_x]})
        for by_z, by_x in farthest_first(
            n_z, n_x, lambda by_z, by_x: ring_distance(by_z, n_z) + ring_distance(by_x, n_x)
        )
    ]
    neighbours = []
    for axis, at, size, odd in (("sub", sub, n_sub, h), ("slab", slab, n_slab, lax.rem(l, 2))):
        after = shifted(at, 1, size)
        before = shifted(at, size - 1, size)
        neighbours.append((axis, 1 - odd, {axis: jnp.where(odd == 1, after, before)}))
        neighbours.append((axis, odd, {axis: jnp.where(odd == 1, before, after)}))
    previous = {"sub": {"sub": shifted(sub, n_sub - 1, n_sub)}, "slab": {"slab": shifted(slab, n_slab - 1, n_slab)}}

    load_speeds = pltpu.make_async_copy(speeds_hbm, speeds, load_sem.at[FIELDS])
    load_speeds.start()
    loads = []
    for f in range(FIELDS):
        load = pltpu.make_async_copy(fields_hbm.at[f], state.at[0, f], load_sem.at[f])
        load.start()
        loads.append(load)

    barrier = pltpu.get_barrier_semaphore()
    greeted = [device for _, _, device in neighbours] + [device for _, device in far + near]
    for device in greeted:
        pl.semaphore_signal(barrier, inc=1, device_id=device, device_id_type=MESH)
    load_speeds.wait()
    for r in range(ROWS):
        speed_send[r : r + 1, :] = speeds[1, r, 0:1, :]
    pl.semaphore_wait(barrier, len(greeted))

    speed_y = pltpu.make_async_remote_copy(
        src_ref=speed_send,
        dst_ref=speed_recv_y,
        send_sem=speed_send_sem.at[0],
        recv_sem=speed_recv_sem.at[0],
        device_id=previous["sub"],
        device_id_type=MESH,
    )
    speed_x = pltpu.make_async_remote_copy(
        src_ref=speeds.at[0, 0],
        dst_ref=speed_recv_x,
        send_sem=speed_send_sem.at[1],
        recv_sem=speed_recv_sem.at[1],
        device_id=previous["slab"],
        device_id_type=MESH,
    )
    speed_y.start()
    speed_x.start()

    def face_copies(n, with_bounds):
        copies = []
        for slot, (axis, way, device) in enumerate(neighbours):
            if axis == "sub":
                sent, received, size = send_y, recv_y, Y_USED if with_bounds else Y_NODES
            else:
                sent, received, size = send_x, recv_x, X_TILES if with_bounds else X_NODES
            copies.append(
                pltpu.make_async_remote_copy(
                    src_ref=sent.at[n, way, pl.ds(0, size)],
                    dst_ref=received.at[n, way, pl.ds(0, size)],
                    send_sem=face_send_sem.at[n, slot],
                    recv_sem=face_recv_sem.at[n, slot],
                    device_id=device,
                    device_id_type=MESH,
                )
            )
        return copies

    def for_faces(n, part, action):
        @pl.when(part == 0)
        def _():
            for copy in face_copies(n, True):
                action(copy)

        @pl.when(part != 0)
        def _():
            for copy in face_copies(n, False):
                action(copy)

    def pack_faces(n, r, values):
        for i in range(3):
            for j in range(3):
                for k in range(3):
                    v = values[i][j][k]
                    if i == 2 and r == ROWS - 1:
                        send_x[n, 0, 3 * j + k] = v
                    if i == 0 and r == 0:
                        send_x[n, 1, 3 * j + k] = v
                    at = 9 * r + 3 * i + k
                    if j == 2:
                        send_y[n, 0, at : at + 1, :] = v[7:8, :]
                    if j == 0:
                        send_y[n, 1, at : at + 1, :] = v[0:1, :]

    def pack_bounds(n, f, r, lowest, highest):
        for which, v in ((0, lowest), (1, highest)):
            bounds[f, r, which] = v
            if r == ROWS - 1:
                send_x[n, 0, 9 + which] = v
            if r == 0:
                send_x[n, 1, 9 + which] = v
            at = 18 + 2 * r + which
            send_y[n, 0, at : at + 1, :] = v[7:8, :]
            send_y[n, 1, at : at + 1, :] = v[0:1, :]

    def first_faces(f, _):
        for r in range(ROWS):
            values = [
                [[state[0, f, i, j, k, r] for k in range(3)] for j in range(3)] for i in range(3)
            ]
            flat = [values[i][j][k] for i in range(3) for j in range(3) for k in range(3)]
            pack_faces(f, r, values)
            pack_bounds(
                f, f, r, tree(jnp.minimum, flat), tree(jnp.maximum, flat)
            )
        for copy in face_copies(f, True):
            copy.start()
        return 0

    for load in loads:
        load.wait()
    lax.fori_loop(0, FIELDS, first_faces, 0)

    row_at = lax.broadcasted_iota(jnp.int32, (8, 128), 0)
    at_bottom = row_at == 0
    at_top = row_at == 7

    speed_y.wait_recv()
    speed_x.wait_recv()
    face_x = [speeds[0, r] for r in range(ROWS)] + [speed_recv_x[...]]
    y_lo = [speeds[1, r] for r in range(ROWS)]
    y_hi = [
        jnp.where(
            at_top,
            jnp.broadcast_to(speed_recv_y[r : r + 1, :], (8, 128)),
            pltpu.roll(y_lo[r], 7, 0),
        )
        for r in range(ROWS)
    ]
    z_lo = [speeds[2, r] for r in range(ROWS)]
    interiors = [
        [0.5 * (face_x[r] + face_x[r + 1]) for r in range(ROWS)],
        [0.5 * (y_lo[r] + y_hi[r]) for r in range(ROWS)],
        [0.5 * (z_lo[r] + pltpu.roll(z_lo[r], 127, 1)) for r in range(ROWS)],
    ]
    fast = None
    for r in range(ROWS):
        total = jnp.abs(interiors[0][r]) + jnp.abs(interiors[1][r]) + jnp.abs(interiors[2][r])
        fast = total if fast is None else jnp.maximum(fast, total)
    fast = jnp.max(fast, axis=0, keepdims=True)
    def coefficients():
        up = lambda s: 6.0 * jnp.maximum(s, 0.0)
        down = lambda s: 6.0 * jnp.minimum(s, 0.0)
        tiles = [-interiors[d][r] for r in range(ROWS) for d in range(3)]
        for r in range(ROWS):
            y_up, y_down = up(y_lo[r]), down(y_hi[r])
            tiles += [
                jnp.where(at_bottom, 0.0, y_up),
                down(y_lo[r]),
                up(y_hi[r]),
                jnp.where(at_top, 0.0, y_down),
                up(z_lo[r]),
                down(z_lo[r]),
                jnp.where(at_bottom, y_up, 0.0),
                jnp.where(at_top, y_down, 0.0),
            ]
        for q in range(ROWS + 1):
            tiles += [up(face_x[q]), down(face_x[q])]
        return tiles

    def shares(t):
        part = lax.rem(t, 3)
        pick = lambda *values: jnp.where(
            part == 0, values[0], jnp.where(part == 1, values[1], values[2])
        ).astype(jnp.float32)
        return pick(0.0, 0.75, 1.0 / 3.0), pick(1.0, 0.25, 2.0 / 3.0)

    def inner_part(t, f, rate_only=False):
        source = lax.rem(t, 3)
        share, rest = shares(t)
        for r in range(ROWS):
            v = [
                [[state[source, f, i, j, k, r] for k in range(3)] for j in range(3)]
                for i in range(3)
            ]
            new = [
                [[None if rate_only else v[i][j][k] for k in range(3)] for j in range(3)]
                for i in range(3)
            ]
            a = [coef[3 * r + d] for d in range(3)]
            up_x = [coef[22 + 2 * q] for q in (r, r + 1)]
            down_x = [coef[23 + 2 * q] for q in (r, r + 1)]
            up_y, down_y, up_y_hi, down_y_hi, up_z, down_z = [coef[6 + 8 * r + n] for n in range(6)]
            for k in range(3):
                for j in range(3):
                    flux_lo = down_x[0] * v[0][j][k]
                    if r > 0:
                        flux_lo = flux_lo + up_x[0] * state[source, f, 2, j, k, r - 1]
                    flux_hi = up_x[1] * v[2][j][k]
                    if r < ROWS - 1:
                        flux_hi = flux_hi + down_x[1] * state[source, f, 0, j, k, r + 1]
                    terms = line_terms(v[0][j][k], v[1][j][k], v[2][j][k], a[0], flux_lo, flux_hi)
                    for i in range(3):
                        new[i][j][k] = terms[i] if rate_only else new[i][j][k] + terms[i]
                for i in range(3):
                    flux_lo = up_y * pltpu.roll(v[i][2][k], 1, 0) + down_y * v[i][0][k]
                    flux_hi = up_y_hi * v[i][2][k] + down_y_hi * pltpu.roll(v[i][0][k], 7, 0)
                    terms = line_terms(v[i][0][k], v[i][1][k], v[i][2][k], a[1], flux_lo, flux_hi)
                    for j in range(3):
                        new[i][j][k] = new[i][j][k] + terms[j]
            for i in range(3):
                for j in range(3):
                    flux_lo = up_z * pltpu.roll(v[i][j][2], 1, 1) + down_z * v[i][j][0]
                    flux_hi = pltpu.roll(flux_lo, 127, 1)
                    terms = line_terms(v[i][j][0], v[i][j][1], v[i][j][2], a[2], flux_lo, flux_hi)
                    for k in range(3):
                        x = new[i][j][k] + terms[k]
                        if not rate_only:
                            x = share * state[0, f, i, j, k, r] + rest * x
                        partial[f, i, j, k, r] = x

    for phase, (received, partners) in enumerate(((near_max, near), (far_max, far))):
        n = received.shape[0]
        received[0] = fast
        if n > 1:
            max_send[phase] = fast
            for slot, device in partners:
                copy = pltpu.make_async_remote_copy(
                    src_ref=max_send.at[phase],
                    dst_ref=received.at[slot],
                    send_sem=max_send_sem.at[phase],
                    recv_sem=max_recv_sem.at[phase],
                    device_id=device,
                    device_id_type=MESH,
                )
                copy.start()
            if phase == 0:
                for at, v in enumerate(coefficients()):
                    coef[at] = v
                lax.fori_loop(0, FIELDS, lambda f, _: (inner_part(0, f, True), 0)[1], 0)
            pltpu.make_async_copy(
                received.at[pl.ds(1, n - 1)], received.at[pl.ds(1, n - 1)], max_recv_sem.at[phase]
            ).wait()
            fast = jnp.max(received[...], axis=0)
    fastest = jnp.max(jnp.broadcast_to(fast, (8, 128)), axis=1, keepdims=True)
    time_step = COURANT / (jnp.broadcast_to(fastest, (8, 128)) + 1e-6)
    for at in range(coef.shape[0]):
        coef[at] = time_step * coef[at]

    def begin(f):
        for r in range(ROWS):
            for i in range(3):
                for j in range(3):
                    for k in range(3):
                        at = (f, i, j, k, r)
                        partial[at] = state[(0, *at)] + time_step * partial[at]

    def spread(row):
        return jnp.broadcast_to(row, (8, 128))

    def gather_bounds(n, f):
        for at, pick in ((0, jnp.minimum), (1, jnp.maximum)):
            values = [bounds[f, r, at] for r in range(ROWS)]
            ring = [recv_x[n, 0, 9 + at]] + values + [recv_x[n, 1, 9 + at]]
            for r in range(ROWS):
                here = 18 + 2 * r + at
                v = values[r]
                below = jnp.where(
                    at_bottom, spread(recv_y[n, 0, here : here + 1, :]), pltpu.roll(v, 1, 0)
                )
                above = jnp.where(
                    at_top, spread(recv_y[n, 1, here : here + 1, :]), pltpu.roll(v, 7, 0)
                )
                best = pick(pick(v, ring[r]), ring[r + 2])
                best = pick(best, pick(below, above))
                best = pick(best, pick(pltpu.roll(v, 1, 1), pltpu.roll(v, 127, 1)))
                bounds[f, r, 2 + at] = best

    def outer_part(n, t, f):
        target = lax.rem(t + 1, 3)
        _, rest = shares(t)
        for r in range(ROWS):
            x = [
                [[partial[f, i, j, k, r] for k in range(3)] for j in range(3)] for i in range(3)
            ]
            up_y, down_y = [rest * coef[12 + 8 * r + n] for n in range(2)]
            for k in range(3):
                for j in range(3):
                    if r == 0:
                        up_x = rest * coef[22]
                        x[0][j][k] = x[0][j][k] + up_x * recv_x[n, 0, 3 * j + k]
                    if r == ROWS - 1:
                        down_x = rest * coef[23 + 2 * ROWS]
                        x[2][j][k] = x[2][j][k] - down_x * recv_x[n, 1, 3 * j + k]
                for i in range(3):
                    at = 9 * r + 3 * i + k
                    x[i][0][k] = x[i][0][k] + up_y * spread(recv_y[n, 0, at : at + 1, :])
                    x[i][2][k] = x[i][2][k] - down_y * spread(recv_y[n, 1, at : at + 1, :])
            averages, tops, bottoms = [], [], []
            for i in range(3):
                for j in range(3):
                    lo, mid, hi = x[i][j]
                    tops.append(jnp.maximum(jnp.maximum(lo, hi), mid))
                    bottoms.append(jnp.minimum(jnp.minimum(lo, hi), mid))
                    line = (lo + hi) + 4.0 * mid
                    weight = NODE_WEIGHTS[i] * NODE_WEIGHTS[j]
                    averages.append(line if weight == 1.0 else weight * line)
            average = tree(jnp.add, averages) * (1.0 / 216.0)
            largest = tree(jnp.maximum, tops)
            smallest = tree(jnp.minimum, bottoms)
            lowest = bounds[f, r, 2]
            highest = bounds[f, r, 3]
            upper = (jnp.maximum(highest - average, 0.0) + SOFTNESS) / (largest - average + SOFTNESS)
            lower = (jnp.maximum(average - lowest, 0.0) + SOFTNESS) / (average - smallest + SOFTNESS)
            scaling = jnp.minimum(1.0, jnp.minimum(upper, lower))
            offset = average - scaling * average
            for i in range(3):
                for j in range(3):
                    for k in range(3):
                        x[i][j][k] = scaling * x[i][j][k] + offset
                        state[target, f, i, j, k, r] = x[i][j][k]
            pack_faces(n + FIELDS, r, x)
            pack_bounds(n + FIELDS, f, r, scaling * smallest + offset, scaling * largest + offset)

    def stage(n, _):
        t = lax.div(n, FIELDS)
        f = n - FIELDS * t
        part = lax.rem(t, 3)

        @pl.when(t == 0)
        def _():
            begin(f)

        for_faces(n, part, lambda copy: copy.wait_recv())

        @pl.when(part == 0)
        def _():
            gather_bounds(n, f)

        outer_part(n, t, f)

        @pl.when(t < STAGES - 1)
        def _():
            for_faces(n + FIELDS, lax.rem(part + 1, 3), lambda copy: copy.start())
            inner_part(t + 1, f)

        @pl.when(t == STAGES - 1)
        def _():
            pltpu.make_async_copy(state.at[0, f], out_hbm.at[f], store_sem.at[f]).start()

        return 0

    lax.fori_loop(0, STAGES * FIELDS, stage, 0)

    speed_y.wait_send()
    speed_x.wait_send()
    for phase, received in enumerate((near_max, far_max)):
        n = received.shape[0]
        if n > 1:
            pltpu.make_async_copy(
                received.at[pl.ds(1, n - 1)], received.at[pl.ds(1, n - 1)], max_send_sem.at[phase]
            ).wait()

    def drain(n, _):
        for_faces(n, lax.rem(lax.div(n, FIELDS), 3), lambda copy: copy.wait_send())
        return 0

    lax.fori_loop(0, STAGES * FIELDS, drain, 0)
    for f in range(FIELDS):
        pltpu.make_async_copy(state.at[0, f], out_hbm.at[f], store_sem.at[f]).wait()


def solution(mesh):
    n_slab, n_sub = mesh.shape["slab"], mesh.shape["sub"]
    n_near = 16
    n_far = n_slab * n_sub // n_near

    def on_device(fields, speeds):
        vmem = lambda *shape: pltpu.VMEM(shape, jnp.float32)
        dma = lambda *shape: pltpu.SemaphoreType.DMA(shape)
        return pl.pallas_call(
            functools.partial(kernel, n_slab, n_sub),
            out_shape=jax.ShapeDtypeStruct(fields.shape, fields.dtype),
            in_specs=[pl.BlockSpec(memory_space=pltpu.HBM)] * 2,
            out_specs=pl.BlockSpec(memory_space=pl.ANY),
            scratch_shapes=[
                vmem(3, FIELDS, 3, 3, 3, ROWS, 8, 128),
                vmem(FIELDS, 3, 3, 3, ROWS, 8, 128),
                vmem(3, ROWS, 8, 128),
                vmem(FIELDS, ROWS, 4, 8, 128),
                vmem(24 + 2 * ROWS, 8, 128),
                vmem((STAGES + 1) * FIELDS, 2, X_TILES, 8, 128),
                vmem(STAGES * FIELDS, 2, X_TILES, 8, 128),
                vmem((STAGES + 1) * FIELDS, 2, Y_ROWS, 128),
                vmem(STAGES * FIELDS, 2, Y_ROWS, 128),
                vmem(8, 128),
                vmem(8, 128),
                vmem(8, 128),
                vmem(n_near, 1, 128),
                vmem(n_far, 1, 128),
                vmem(2, 1, 128),
                dma(FIELDS + 1),
                dma(FIELDS),
                dma(STAGES * FIELDS, 4),
                dma(STAGES * FIELDS, 4),
                dma(2),
                dma(2),
                dma(2),
                dma(2),
            ],
            compiler_params=pltpu.CompilerParams(
                collective_id=1, has_side_effects=True, vmem_limit_bytes=60 * 1024 * 1024
            ),
            name="remap",
        )(fields, speeds)

    spec = P(None, None, None, None, "slab", "sub", None)
    return jax.shard_map(
        on_device,
        mesh=mesh,
        in_specs=(spec, P(None, "slab", "sub", None)),
        out_specs=spec,
        check_vma=False,
    )
```

```python
import functools

import jax
import jax.numpy as jnp
from jax import lax
from jax.experimental import pallas as pl
from jax.experimental.pallas import tpu as pltpu
from jax.sharding import PartitionSpec as P

STEPS = 3
STAGES = 3 * STEPS
FIELDS = 3
ROWS = 2
COURANT = 0.12
SOFTNESS = 0.05
NODE_WEIGHTS = (1.0, 4.0, 1.0)
MESH = pl.DeviceIdType.MESH
X_TILES, X_NODES = 11, 9
Y_ROWS, Y_USED, Y_NODES = 24, 22, 18


def ring_distance(by, size):
    return min(by, size - by)


def farthest_first(outer, inner, hops):
    steps = [(a, b) for a in range(outer) for b in range(inner) if a or b]
    return sorted(steps, key=lambda step: -hops(*step))


def tree(pick, values):
    while len(values) > 1:
        values = [
            pick(values[n], values[n + 1]) if n + 1 < len(values) else values[n]
            for n in range(0, len(values), 2)
        ]
    return values[0]


def line_terms(v0, v1, v2, a, flux_lo, flux_hi):
    d = v2 - v0
    t = (v0 + v2) + 4.0 * v1
    big = a * t
    small = a * d
    twice = small + small
    return (big - twice) + flux_lo, small, -((big + twice) + flux_hi)


def kernel(
    n_slab,
    n_sub,
    fields_hbm,
    speeds_hbm,
    out,
    state,
    partial,
    speeds,
    bounds,
    coef,
    send_x,
    recv_x,
    send_y,
    recv_y,
    speed_send,
    speed_recv_x,
    speed_recv_y,
    near_max,
    far_max,
    max_send,
    measure,
    load_sem,
    face_send_sem,
    face_recv_sem,
    speed_send_sem,
    speed_recv_sem,
    max_send_sem,
    max_recv_sem,
):
    slab = lax.axis_index("slab")
    sub = lax.axis_index("sub")
    n_z, n_x = n_slab // 8, n_sub // 2

    def shifted(at, by, size):
        moved = at + by
        return jnp.where(moved >= size, moved - size, moved)

    z, l = lax.div(slab, 8), lax.rem(slab, 8)
    x, h = lax.div(sub, 2), lax.rem(sub, 2)
    along_l = [8 * z + shifted(l, by, 8) for by in range(8)]
    along_h = [2 * x + shifted(h, by, 2) for by in range(2)]
    along_z = [8 * shifted(z, by, n_z) + l for by in range(n_z)]
    along_x = [2 * shifted(x, by, n_x) + h for by in range(n_x)]
    near = [
        (2 * by_l + by_h, {"slab": along_l[by_l], "sub": along_h[by_h]})
        for by_h, by_l in farthest_first(
            2, 8, lambda by_h, by_l: ring_distance((4 * by_h + by_l // 2) % 8, 8)
        )
    ]
    far = [
        (n_x * by_z + by_x, {"slab": along_z[by_z], "sub": along_x[by_x]})
        for by_z, by_x in farthest_first(
            n_z, n_x, lambda by_z, by_x: ring_distance(by_z, n_z) + ring_distance(by_x, n_x)
        )
    ]
    neighbours = []
    for axis, at, size, odd in (("sub", sub, n_sub, h), ("slab", slab, n_slab, lax.rem(l, 2))):
        after = shifted(at, 1, size)
        before = shifted(at, size - 1, size)
        neighbours.append((axis, 1 - odd, {axis: jnp.where(odd == 1, after, before)}))
        neighbours.append((axis, odd, {axis: jnp.where(odd == 1, before, after)}))
    previous = {"sub": {"sub": shifted(sub, n_sub - 1, n_sub)}, "slab": {"slab": shifted(slab, n_slab - 1, n_slab)}}

    load_speeds = pltpu.make_async_copy(speeds_hbm, speeds, load_sem.at[0])
    load_speeds.start()
    load_fields = pltpu.make_async_copy(fields_hbm, state.at[0], load_sem.at[1])
    load_fields.start()

    barrier = pltpu.get_barrier_semaphore()
    greeted = [device for _, _, device in neighbours] + [device for _, device in far + near]
    for device in greeted:
        pl.semaphore_signal(barrier, inc=1, device_id=device, device_id_type=MESH)
    load_speeds.wait()
    for r in range(ROWS):
        speed_send[r : r + 1, :] = speeds[1, r, 0:1, :]
    pl.semaphore_wait(barrier, len(greeted))

    speed_y = pltpu.make_async_remote_copy(
        src_ref=speed_send,
        dst_ref=speed_recv_y,
        send_sem=speed_send_sem.at[0],
        recv_sem=speed_recv_sem.at[0],
        device_id=previous["sub"],
        device_id_type=MESH,
    )
    speed_x = pltpu.make_async_remote_copy(
        src_ref=speeds.at[0, 0],
        dst_ref=speed_recv_x,
        send_sem=speed_send_sem.at[1],
        recv_sem=speed_recv_sem.at[1],
        device_id=previous["slab"],
        device_id_type=MESH,
    )
    speed_y.start()
    speed_x.start()

    def face_copies(n, with_bounds):
        copies = []
        for axis, way, device in neighbours:
            if axis == "sub":
                sent, received, size = send_y, recv_y, Y_USED if with_bounds else Y_NODES
            else:
                sent, received, size = send_x, recv_x, X_TILES if with_bounds else X_NODES
            copies.append(
                pltpu.make_async_remote_copy(
                    src_ref=sent.at[n, way, pl.ds(0, size)],
                    dst_ref=received.at[n, way, pl.ds(0, size)],
                    send_sem=face_send_sem.at[lax.rem(n, 2 * FIELDS)],
                    recv_sem=face_recv_sem.at[lax.rem(n, 2 * FIELDS)],
                    device_id=device,
                    device_id_type=MESH,
                )
            )
        return copies

    def start_faces(n, part):
        @pl.when(part == 0)
        def _():
            for copy in face_copies(n, True):
                copy.start()

        @pl.when(part != 0)
        def _():
            for copy in face_copies(n, False):
                copy.start()

    def wait_rows(rows, sem):
        pltpu.make_async_copy(measure.at[pl.ds(0, rows)], measure.at[pl.ds(0, rows)], sem).wait()

    def wait_faces(n, part, sems):
        @pl.when(part == 0)
        def _():
            wait_rows(2 * (Y_USED + 8 * X_TILES), sems.at[lax.rem(n, 2 * FIELDS)])

        @pl.when(part != 0)
        def _():
            wait_rows(2 * (Y_NODES + 8 * X_NODES), sems.at[lax.rem(n, 2 * FIELDS)])

    def pack_faces(n, r, values):
        for i in range(3):
            for j in range(3):
                for k in range(3):
                    v = values[i][j][k]
                    if i == 2 and r == ROWS - 1:
                        send_x[n, 0, 3 * j + k] = v
                    if i == 0 and r == 0:
                        send_x[n, 1, 3 * j + k] = v
                    at = 9 * r + 3 * i + k
                    if j == 2:
                        send_y[n, 0, at : at + 1, :] = v[7:8, :]
                    if j == 0:
                        send_y[n, 1, at : at + 1, :] = v[0:1, :]

    def pack_bounds(n, f, r, lowest, highest):
        for which, v in ((0, lowest), (1, highest)):
            bounds[f, r, which] = v
            if r == ROWS - 1:
                send_x[n, 0, 9 + which] = v
            if r == 0:
                send_x[n, 1, 9 + which] = v
            at = 18 + 2 * r + which
            send_y[n, 0, at : at + 1, :] = v[7:8, :]
            send_y[n, 1, at : at + 1, :] = v[0:1, :]

    def first_faces(f, _):
        for r in range(ROWS):
            values = [
                [[state[0, f, i, j, k, r] for k in range(3)] for j in range(3)] for i in range(3)
            ]
            flat = [values[i][j][k] for i in range(3) for j in range(3) for k in range(3)]
            pack_faces(f, r, values)
            pack_bounds(
                f, f, r, tree(jnp.minimum, flat), tree(jnp.maximum, flat)
            )
        for copy in face_copies(f, True):
            copy.start()
        return 0

    load_fields.wait()
    lax.fori_loop(0, FIELDS, first_faces, 0)

    row_at = lax.broadcasted_iota(jnp.int32, (8, 128), 0)
    at_bottom = row_at == 0
    at_top = row_at == 7

    speed_y.wait_recv()
    speed_x.wait_recv()
    face_x = [speeds[0, r] for r in range(ROWS)] + [speed_recv_x[...]]
    y_lo = [speeds[1, r] for r in range(ROWS)]
    y_hi = [
        jnp.where(
            at_top,
            jnp.broadcast_to(speed_recv_y[r : r + 1, :], (8, 128)),
            pltpu.roll(y_lo[r], 7, 0),
        )
        for r in range(ROWS)
    ]
    z_lo = [speeds[2, r] for r in range(ROWS)]
    interiors = [
        [0.5 * (face_x[r] + face_x[r + 1]) for r in range(ROWS)],
        [0.5 * (y_lo[r] + y_hi[r]) for r in range(ROWS)],
        [0.5 * (z_lo[r] + pltpu.roll(z_lo[r], 127, 1)) for r in range(ROWS)],
    ]
    fast = None
    for r in range(ROWS):
        total = jnp.abs(interiors[0][r]) + jnp.abs(interiors[1][r]) + jnp.abs(interiors[2][r])
        fast = total if fast is None else jnp.maximum(fast, total)
    fast = jnp.max(fast, axis=0, keepdims=True)
    def coefficients():
        up = lambda s: 6.0 * jnp.maximum(s, 0.0)
        down = lambda s: 6.0 * jnp.minimum(s, 0.0)
        tiles = [-interiors[d][r] for r in range(ROWS) for d in range(3)]
        for r in range(ROWS):
            y_up, y_down = up(y_lo[r]), down(y_hi[r])
            tiles += [
                jnp.where(at_bottom, 0.0, y_up),
                down(y_lo[r]),
                up(y_hi[r]),
                jnp.where(at_top, 0.0, y_down),
                up(z_lo[r]),
                down(z_lo[r]),
                jnp.where(at_bottom, y_up, 0.0),
                jnp.where(at_top, y_down, 0.0),
            ]
        for q in range(ROWS + 1):
            tiles += [up(face_x[q]), down(face_x[q])]
        return tiles

    def shares(t):
        part = lax.rem(t, 3)
        pick = lambda *values: jnp.where(
            part == 0, values[0], jnp.where(part == 1, values[1], values[2])
        ).astype(jnp.float32)
        return pick(0.0, 0.75, 1.0 / 3.0), pick(1.0, 0.25, 2.0 / 3.0)

    def inner_part(t, f, rate_only=False):
        source = lax.rem(t, 3)
        share, rest = shares(t)
        for r in range(ROWS):
            v = [
                [[state[source, f, i, j, k, r] for k in range(3)] for j in range(3)]
                for i in range(3)
            ]
            new = [
                [[None if rate_only else v[i][j][k] for k in range(3)] for j in range(3)]
                for i in range(3)
            ]
            a = [coef[3 * r + d] for d in range(3)]
            up_x = [coef[22 + 2 * q] for q in (r, r + 1)]
            down_x = [coef[23 + 2 * q] for q in (r, r + 1)]
            up_y, down_y, up_y_hi, down_y_hi, up_z, down_z = [coef[6 + 8 * r + n] for n in range(6)]
            for k in range(3):
                for j in range(3):
                    flux_lo = down_x[0] * v[0][j][k]
                    if r > 0:
                        flux_lo = flux_lo + up_x[0] * state[source, f, 2, j, k, r - 1]
                    flux_hi = up_x[1] * v[2][j][k]
                    if r < ROWS - 1:
                        flux_hi = flux_hi + down_x[1] * state[source, f, 0, j, k, r + 1]
                    terms = line_terms(v[0][j][k], v[1][j][k], v[2][j][k], a[0], flux_lo, flux_hi)
                    for i in range(3):
                        new[i][j][k] = terms[i] if rate_only else new[i][j][k] + terms[i]
                for i in range(3):
                    flux_lo = up_y * pltpu.roll(v[i][2][k], 1, 0) + down_y * v[i][0][k]
                    flux_hi = up_y_hi * v[i][2][k] + down_y_hi * pltpu.roll(v[i][0][k], 7, 0)
                    terms = line_terms(v[i][0][k], v[i][1][k], v[i][2][k], a[1], flux_lo, flux_hi)
                    for j in range(3):
                        new[i][j][k] = new[i][j][k] + terms[j]
            for i in range(3):
                for j in range(3):
                    flux_lo = up_z * pltpu.roll(v[i][j][2], 1, 1) + down_z * v[i][j][0]
                    flux_hi = pltpu.roll(flux_lo, 127, 1)
                    terms = line_terms(v[i][j][0], v[i][j][1], v[i][j][2], a[2], flux_lo, flux_hi)
                    for k in range(3):
                        x = new[i][j][k] + terms[k]
                        if not rate_only:
                            x = share * state[0, f, i, j, k, r] + rest * x
                        partial[f, i, j, k, r] = x

    for phase, (received, partners) in enumerate(((near_max, near), (far_max, far))):
        n = received.shape[0]
        received[0] = fast
        if n > 1:
            max_send[phase] = fast
            for slot, device in partners:
                copy = pltpu.make_async_remote_copy(
                    src_ref=max_send.at[phase],
                    dst_ref=received.at[slot],
                    send_sem=max_send_sem.at[phase],
                    recv_sem=max_recv_sem.at[phase],
                    device_id=device,
                    device_id_type=MESH,
                )
                copy.start()
            if phase == 0:
                for at, v in enumerate(coefficients()):
                    coef[at] = v
                lax.fori_loop(0, FIELDS, lambda f, _: (inner_part(0, f, True), 0)[1], 0)
            pltpu.make_async_copy(
                received.at[pl.ds(1, n - 1)], received.at[pl.ds(1, n - 1)], max_recv_sem.at[phase]
            ).wait()
            fast = jnp.max(received[...], axis=0)
    fastest = jnp.max(jnp.broadcast_to(fast, (8, 128)), axis=1, keepdims=True)
    time_step = COURANT / (jnp.broadcast_to(fastest, (8, 128)) + 1e-6)
    for at in range(coef.shape[0]):
        coef[at] = time_step * coef[at]

    def begin(f):
        for r in range(ROWS):
            for i in range(3):
                for j in range(3):
                    for k in range(3):
                        at = (f, i, j, k, r)
                        partial[at] = state[(0, *at)] + time_step * partial[at]

    def spread(row):
        return jnp.broadcast_to(row, (8, 128))

    def gather_bounds(n, f):
        for at, pick in ((0, jnp.minimum), (1, jnp.maximum)):
            values = [bounds[f, r, at] for r in range(ROWS)]
            ring = [recv_x[n, 0, 9 + at]] + values + [recv_x[n, 1, 9 + at]]
            for r in range(ROWS):
                here = 18 + 2 * r + at
                v = values[r]
                below = jnp.where(
                    at_bottom, spread(recv_y[n, 0, here : here + 1, :]), pltpu.roll(v, 1, 0)
                )
                above = jnp.where(
                    at_top, spread(recv_y[n, 1, here : here + 1, :]), pltpu.roll(v, 7, 0)
                )
                best = pick(pick(v, ring[r]), ring[r + 2])
                best = pick(best, pick(below, above))
                best = pick(best, pick(pltpu.roll(v, 1, 1), pltpu.roll(v, 127, 1)))
                bounds[f, r, 2 + at] = best

    def outer_part(n, t, f):
        target = lax.rem(t + 1, 3)
        _, rest = shares(t)
        for r in range(ROWS):
            x = [
                [[partial[f, i, j, k, r] for k in range(3)] for j in range(3)] for i in range(3)
            ]
            up_y, down_y = [rest * coef[12 + 8 * r + n] for n in range(2)]
            for k in range(3):
                for j in range(3):
                    if r == 0:
                        up_x = rest * coef[22]
                        x[0][j][k] = x[0][j][k] + up_x * recv_x[n, 0, 3 * j + k]
                    if r == ROWS - 1:
                        down_x = rest * coef[23 + 2 * ROWS]
                        x[2][j][k] = x[2][j][k] - down_x * recv_x[n, 1, 3 * j + k]
                for i in range(3):
                    at = 9 * r + 3 * i + k
                    x[i][0][k] = x[i][0][k] + up_y * spread(recv_y[n, 0, at : at + 1, :])
                    x[i][2][k] = x[i][2][k] - down_y * spread(recv_y[n, 1, at : at + 1, :])
            averages, tops, bottoms = [], [], []
            for i in range(3):
                for j in range(3):
                    lo, mid, hi = x[i][j]
                    tops.append(jnp.maximum(jnp.maximum(lo, hi), mid))
                    bottoms.append(jnp.minimum(jnp.minimum(lo, hi), mid))
                    line = (lo + hi) + 4.0 * mid
                    weight = NODE_WEIGHTS[i] * NODE_WEIGHTS[j]
                    averages.append(line if weight == 1.0 else weight * line)
            average = tree(jnp.add, averages) * (1.0 / 216.0)
            largest = tree(jnp.maximum, tops)
            smallest = tree(jnp.minimum, bottoms)
            lowest = bounds[f, r, 2]
            highest = bounds[f, r, 3]
            upper = (jnp.maximum(highest - average, 0.0) + SOFTNESS) / (largest - average + SOFTNESS)
            lower = (jnp.maximum(average - lowest, 0.0) + SOFTNESS) / (average - smallest + SOFTNESS)
            scaling = jnp.minimum(1.0, jnp.minimum(upper, lower))
            offset = average - scaling * average
            for i in range(3):
                for j in range(3):
                    for k in range(3):
                        x[i][j][k] = scaling * x[i][j][k] + offset
                        state[target, f, i, j, k, r] = x[i][j][k]
            pack_faces(n + FIELDS, r, x)
            pack_bounds(n + FIELDS, f, r, scaling * smallest + offset, scaling * largest + offset)

    def stage(n, _):
        t = lax.div(n, FIELDS)
        f = n - FIELDS * t
        part = lax.rem(t, 3)

        @pl.when(t == 0)
        def _():
            begin(f)

        wait_faces(n, part, face_recv_sem)

        @pl.when(part == 0)
        def _():
            gather_bounds(n, f)

        outer_part(n, t, f)

        @pl.when(t < STAGES - 1)
        def _():
            start_faces(n + FIELDS, lax.rem(part + 1, 3))
            inner_part(t + 1, f)

        wait_faces(n, part, face_send_sem)

        @pl.when(t == STAGES - 1)
        def _():
            out[f] = state[0, f]

        return 0

    speed_y.wait_send()
    speed_x.wait_send()
    for phase, received in enumerate((near_max, far_max)):
        n = received.shape[0]
        if n > 1:
            pltpu.make_async_copy(
                received.at[pl.ds(1, n - 1)], received.at[pl.ds(1, n - 1)], max_send_sem.at[phase]
            ).wait()

    lax.fori_loop(0, STAGES * FIELDS, stage, 0)


def solution(mesh):
    n_slab, n_sub = mesh.shape["slab"], mesh.shape["sub"]
    n_near = 16
    n_far = n_slab * n_sub // n_near

    def on_device(fields, speeds):
        vmem = lambda *shape: pltpu.VMEM(shape, jnp.float32)
        dma = lambda *shape: pltpu.SemaphoreType.DMA(shape)
        return pl.pallas_call(
            functools.partial(kernel, n_slab, n_sub),
            out_shape=pltpu.VMEM(fields.shape, fields.dtype),
            in_specs=[pl.BlockSpec(memory_space=pltpu.HBM)] * 2,
            out_specs=pl.BlockSpec(memory_space=pltpu.VMEM),
            scratch_shapes=[
                vmem(3, FIELDS, 3, 3, 3, ROWS, 8, 128),
                vmem(FIELDS, 3, 3, 3, ROWS, 8, 128),
                vmem(3, ROWS, 8, 128),
                vmem(FIELDS, ROWS, 4, 8, 128),
                vmem(24 + 2 * ROWS, 8, 128),
                vmem((STAGES + 1) * FIELDS, 2, X_TILES, 8, 128),
                vmem(STAGES * FIELDS, 2, X_TILES, 8, 128),
                vmem((STAGES + 1) * FIELDS, 2, Y_ROWS, 128),
                vmem(STAGES * FIELDS, 2, Y_ROWS, 128),
                vmem(8, 128),
                vmem(8, 128),
                vmem(8, 128),
                vmem(n_near, 1, 128),
                vmem(n_far, 1, 128),
                vmem(2, 1, 128),
                vmem(2 * (Y_USED + 8 * X_TILES) + 4, 128),
                dma(2),
                dma(2 * FIELDS),
                dma(2 * FIELDS),
                dma(2),
                dma(2),
                dma(2),
                dma(2),
            ],
            compiler_params=pltpu.CompilerParams(
                collective_id=1, has_side_effects=True, vmem_limit_bytes=60 * 1024 * 1024
            ),
            name="remap",
        )(fields, speeds)

    spec = P(None, None, None, None, "slab", "sub", None)
    return jax.shard_map(
        on_device,
        mesh=mesh,
        in_specs=(spec, P(None, "slab", "sub", None)),
        out_specs=spec,
        check_vma=False,
    )
```

```python
import functools

import jax
import jax.numpy as jnp
from jax import lax
from jax.experimental import pallas as pl
from jax.experimental.pallas import tpu as pltpu
from jax.sharding import PartitionSpec as P

STEPS = 3
STAGES = 3 * STEPS
FIELDS = 3
ROWS = 2
COURANT = 0.12
SOFTNESS = 0.05
NODE_WEIGHTS = (1.0, 4.0, 1.0)
MESH = pl.DeviceIdType.MESH
X_TILES, X_NODES = 11, 9
Y_ROWS, Y_USED, Y_NODES = 24, 22, 18


def tree(pick, values):
    while len(values) > 1:
        values = [
            pick(values[n], values[n + 1]) if n + 1 < len(values) else values[n]
            for n in range(0, len(values), 2)
        ]
    return values[0]


def line_terms(v0, v1, v2, a, flux_lo, flux_hi):
    d = v2 - v0
    t = (v0 + v2) + 4.0 * v1
    big = a * t
    small = a * d
    twice = small + small
    return (big - twice) + flux_lo, small, -((big + twice) + flux_hi)


def kernel(
    n_slab,
    n_sub,
    fields_hbm,
    speeds_hbm,
    out,
    state,
    partial,
    speeds,
    bounds,
    coef,
    send_x,
    recv_x,
    send_y,
    recv_y,
    speed_send,
    speed_recv_x,
    speed_recv_y,
    near_max,
    far_max,
    max_send,
    measure,
    load_sem,
    face_send_sem,
    face_recv_sem,
    speed_send_sem,
    speed_recv_sem,
    max_send_sem,
    max_recv_sem,
):
    slab = lax.axis_index("slab")
    sub = lax.axis_index("sub")
    n_z, n_x = n_slab // 8, n_sub // 2

    def shifted(at, by, size):
        moved = at + by
        return jnp.where(moved >= size, moved - size, moved)

    z, l = lax.div(slab, 8), lax.rem(slab, 8)
    x, h = lax.div(sub, 2), lax.rem(sub, 2)
    n_near, n_far = near_max.shape[0], far_max.shape[0]

    def near_device(by):
        at = shifted(8 * h + l, by, n_near)
        half = jnp.where(at >= 8, 1, 0)
        return {"slab": 8 * z + at - 8 * half, "sub": 2 * x + half}

    def far_device(by):
        at = shifted(n_x * z + x, by, n_far)
        plane = lax.div(at, n_x)
        return {"slab": 8 * plane + l, "sub": 2 * (at - n_x * plane) + h}

    def for_partners(n, action):
        def body(step, _):
            away = lax.div(step + 1, 2)
            action(n // 2 + jnp.where(lax.rem(step, 2) == 1, -away, away))
            return 0

        lax.fori_loop(0, n - 1, body, 0)

    neighbours = []
    for axis, at, size, odd in (("sub", sub, n_sub, h), ("slab", slab, n_slab, lax.rem(l, 2))):
        after = shifted(at, 1, size)
        before = shifted(at, size - 1, size)
        neighbours.append((axis, 1 - odd, {axis: jnp.where(odd == 1, after, before)}))
        neighbours.append((axis, odd, {axis: jnp.where(odd == 1, before, after)}))
    previous = {"sub": {"sub": shifted(sub, n_sub - 1, n_sub)}, "slab": {"slab": shifted(slab, n_slab - 1, n_slab)}}


    barrier = pltpu.get_barrier_semaphore()
    def greet(device):
        pl.semaphore_signal(barrier, inc=1, device_id=device, device_id_type=MESH)

    for _, _, device in neighbours:
        greet(device)
    load_speeds = pltpu.make_async_copy(speeds_hbm, speeds, load_sem.at[0])
    load_speeds.start()
    load_fields = pltpu.make_async_copy(fields_hbm, state.at[0], load_sem.at[1])
    load_fields.start()
    for_partners(n_far, lambda by: greet(far_device(by)))
    for_partners(n_near, lambda by: greet(near_device(by)))
    load_speeds.wait()
    for r in range(ROWS):
        speed_send[r : r + 1, :] = speeds[1, r, 0:1, :]
    pl.semaphore_wait(barrier, len(neighbours) + (n_far - 1) + (n_near - 1))

    speed_y = pltpu.make_async_remote_copy(
        src_ref=speed_send,
        dst_ref=speed_recv_y,
        send_sem=speed_send_sem.at[0],
        recv_sem=speed_recv_sem.at[0],
        device_id=previous["sub"],
        device_id_type=MESH,
    )
    speed_x = pltpu.make_async_remote_copy(
        src_ref=speeds.at[0, 0],
        dst_ref=speed_recv_x,
        send_sem=speed_send_sem.at[1],
        recv_sem=speed_recv_sem.at[1],
        device_id=previous["slab"],
        device_id_type=MESH,
    )
    speed_y.start()
    speed_x.start()

    def face_copies(n, with_bounds):
        copies = []
        for axis, way, device in neighbours:
            if axis == "sub":
                sent, received, size = send_y, recv_y, Y_USED if with_bounds else Y_NODES
            else:
                sent, received, size = send_x, recv_x, X_TILES if with_bounds else X_NODES
            copies.append(
                pltpu.make_async_remote_copy(
                    src_ref=sent.at[n, way, pl.ds(0, size)],
                    dst_ref=received.at[n, way, pl.ds(0, size)],
                    send_sem=face_send_sem.at[lax.rem(n, 2 * FIELDS)],
                    recv_sem=face_recv_sem.at[lax.rem(n, 2 * FIELDS)],
                    device_id=device,
                    device_id_type=MESH,
                )
            )
        return copies

    def start_faces(n, part):
        @pl.when(part == 0)
        def _():
            for copy in face_copies(n, True):
                copy.start()

        @pl.when(part != 0)
        def _():
            for copy in face_copies(n, False):
                copy.start()

    def wait_rows(rows, sem):
        pltpu.make_async_copy(measure.at[pl.ds(0, rows)], measure.at[pl.ds(0, rows)], sem).wait()

    def wait_faces(n, part, sems):
        @pl.when(part == 0)
        def _():
            wait_rows(2 * (Y_USED + 8 * X_TILES), sems.at[lax.rem(n, 2 * FIELDS)])

        @pl.when(part != 0)
        def _():
            wait_rows(2 * (Y_NODES + 8 * X_NODES), sems.at[lax.rem(n, 2 * FIELDS)])

    def pack_faces(n, r, values):
        for i in range(3):
            for j in range(3):
                for k in range(3):
                    v = values[i][j][k]
                    if i == 2 and r == ROWS - 1:
                        send_x[n, 0, 3 * j + k] = v
                    if i == 0 and r == 0:
                        send_x[n, 1, 3 * j + k] = v
                    at = 9 * r + 3 * i + k
                    if j == 2:
                        send_y[n, 0, at : at + 1, :] = v[7:8, :]
                    if j == 0:
                        send_y[n, 1, at : at + 1, :] = v[0:1, :]

    def pack_bounds(n, f, r, lowest, highest):
        for which, v in ((0, lowest), (1, highest)):
            bounds[f, r, which] = v
            if r == ROWS - 1:
                send_x[n, 0, 9 + which] = v
            if r == 0:
                send_x[n, 1, 9 + which] = v
            at = 18 + 2 * r + which
            send_y[n, 0, at : at + 1, :] = v[7:8, :]
            send_y[n, 1, at : at + 1, :] = v[0:1, :]

    def first_faces(f, _):
        for r in range(ROWS):
            values = [
                [[state[0, f, i, j, k, r] for k in range(3)] for j in range(3)] for i in range(3)
            ]
            flat = [values[i][j][k] for i in range(3) for j in range(3) for k in range(3)]
            pack_faces(f, r, values)
            pack_bounds(
                f, f, r, tree(jnp.minimum, flat), tree(jnp.maximum, flat)
            )
        return 0

    def send_first(f, _):
        for copy in face_copies(f, True):
            copy.start()
        return 0

    load_fields.wait()
    lax.fori_loop(0, FIELDS, first_faces, 0)

    row_at = lax.broadcasted_iota(jnp.int32, (8, 128), 0)
    at_bottom = row_at == 0
    at_top = row_at == 7

    speed_y.wait_recv()
    speed_x.wait_recv()
    face_x = [speeds[0, r] for r in range(ROWS)] + [speed_recv_x[...]]
    y_lo = [speeds[1, r] for r in range(ROWS)]
    y_hi = [
        jnp.where(
            at_top,
            jnp.broadcast_to(speed_recv_y[r : r + 1, :], (8, 128)),
            pltpu.roll(y_lo[r], 7, 0),
        )
        for r in range(ROWS)
    ]
    z_lo = [speeds[2, r] for r in range(ROWS)]
    interiors = [
        [0.5 * (face_x[r] + face_x[r + 1]) for r in range(ROWS)],
        [0.5 * (y_lo[r] + y_hi[r]) for r in range(ROWS)],
        [0.5 * (z_lo[r] + pltpu.roll(z_lo[r], 127, 1)) for r in range(ROWS)],
    ]
    fast = None
    for r in range(ROWS):
        total = jnp.abs(interiors[0][r]) + jnp.abs(interiors[1][r]) + jnp.abs(interiors[2][r])
        fast = total if fast is None else jnp.maximum(fast, total)
    fast = jnp.max(fast, axis=0, keepdims=True)
    def coefficients():
        up = lambda s: 6.0 * jnp.maximum(s, 0.0)
        down = lambda s: 6.0 * jnp.minimum(s, 0.0)
        tiles = [-interiors[d][r] for r in range(ROWS) for d in range(3)]
        for r in range(ROWS):
            y_up, y_down = up(y_lo[r]), down(y_hi[r])
            tiles += [
                jnp.where(at_bottom, 0.0, y_up),
                down(y_lo[r]),
                up(y_hi[r]),
                jnp.where(at_top, 0.0, y_down),
                up(z_lo[r]),
                down(z_lo[r]),
                jnp.where(at_bottom, y_up, 0.0),
                jnp.where(at_top, y_down, 0.0),
            ]
        for q in range(ROWS + 1):
            tiles += [up(face_x[q]), down(face_x[q])]
        return tiles

    def shares(t):
        part = lax.rem(t, 3)
        pick = lambda *values: jnp.where(
            part == 0, values[0], jnp.where(part == 1, values[1], values[2])
        ).astype(jnp.float32)
        return pick(0.0, 0.75, 1.0 / 3.0), pick(1.0, 0.25, 2.0 / 3.0)

    def inner_part(t, f, rate_only=False):
        source = lax.rem(t, 3)
        share, rest = shares(t)
        for r in range(ROWS):
            v = [
                [[state[source, f, i, j, k, r] for k in range(3)] for j in range(3)]
                for i in range(3)
            ]
            new = [
                [[None if rate_only else v[i][j][k] for k in range(3)] for j in range(3)]
                for i in range(3)
            ]
            a = [coef[3 * r + d] for d in range(3)]
            up_x = [coef[22 + 2 * q] for q in (r, r + 1)]
            down_x = [coef[23 + 2 * q] for q in (r, r + 1)]
            up_y, down_y, up_y_hi, down_y_hi, up_z, down_z = [coef[6 + 8 * r + n] for n in range(6)]
            for k in range(3):
                for j in range(3):
                    flux_lo = down_x[0] * v[0][j][k]
                    if r > 0:
                        flux_lo = flux_lo + up_x[0] * state[source, f, 2, j, k, r - 1]
                    flux_hi = up_x[1] * v[2][j][k]
                    if r < ROWS - 1:
                        flux_hi = flux_hi + down_x[1] * state[source, f, 0, j, k, r + 1]
                    terms = line_terms(v[0][j][k], v[1][j][k], v[2][j][k], a[0], flux_lo, flux_hi)
                    for i in range(3):
                        new[i][j][k] = terms[i] if rate_only else new[i][j][k] + terms[i]
                for i in range(3):
                    flux_lo = up_y * pltpu.roll(v[i][2][k], 1, 0) + down_y * v[i][0][k]
                    flux_hi = up_y_hi * v[i][2][k] + down_y_hi * pltpu.roll(v[i][0][k], 7, 0)
                    terms = line_terms(v[i][0][k], v[i][1][k], v[i][2][k], a[1], flux_lo, flux_hi)
                    for j in range(3):
                        new[i][j][k] = new[i][j][k] + terms[j]
            for i in range(3):
                for j in range(3):
                    flux_lo = up_z * pltpu.roll(v[i][j][2], 1, 1) + down_z * v[i][j][0]
                    flux_hi = pltpu.roll(flux_lo, 127, 1)
                    terms = line_terms(v[i][j][0], v[i][j][1], v[i][j][2], a[2], flux_lo, flux_hi)
                    for k in range(3):
                        x = new[i][j][k] + terms[k]
                        if not rate_only:
                            x = share * state[0, f, i, j, k, r] + rest * x
                        partial[f, i, j, k, r] = x

    for phase, (received, device_of) in enumerate(((near_max, near_device), (far_max, far_device))):
        n = received.shape[0]
        received[0] = fast
        if n > 1:
            max_send[phase] = fast

            def send(by):
                pltpu.make_async_remote_copy(
                    src_ref=max_send.at[phase],
                    dst_ref=received.at[by],
                    send_sem=max_send_sem.at[phase],
                    recv_sem=max_recv_sem.at[phase],
                    device_id=device_of(by),
                    device_id_type=MESH,
                ).start()

            for_partners(n, send)
            if phase == 0:
                lax.fori_loop(0, FIELDS, send_first, 0)
                for at, v in enumerate(coefficients()):
                    coef[at] = v
                lax.fori_loop(0, FIELDS, lambda f, _: (inner_part(0, f, True), 0)[1], 0)
            pltpu.make_async_copy(
                received.at[pl.ds(1, n - 1)], received.at[pl.ds(1, n - 1)], max_recv_sem.at[phase]
            ).wait()
            fast = jnp.max(received[...], axis=0)
    fastest = jnp.max(jnp.broadcast_to(fast, (8, 128)), axis=1, keepdims=True)
    time_step = COURANT / (jnp.broadcast_to(fastest, (8, 128)) + 1e-6)
    for at in range(coef.shape[0]):
        coef[at] = time_step * coef[at]

    def begin(f):
        for r in range(ROWS):
            for i in range(3):
                for j in range(3):
                    for k in range(3):
                        at = (f, i, j, k, r)
                        partial[at] = state[(0, *at)] + time_step * partial[at]

    def spread(row):
        return jnp.broadcast_to(row, (8, 128))

    def gather_bounds(n, f):
        for at, pick in ((0, jnp.minimum), (1, jnp.maximum)):
            values = [bounds[f, r, at] for r in range(ROWS)]
            ring = [recv_x[n, 0, 9 + at]] + values + [recv_x[n, 1, 9 + at]]
            for r in range(ROWS):
                here = 18 + 2 * r + at
                v = values[r]
                below = jnp.where(
                    at_bottom, spread(recv_y[n, 0, here : here + 1, :]), pltpu.roll(v, 1, 0)
                )
                above = jnp.where(
                    at_top, spread(recv_y[n, 1, here : here + 1, :]), pltpu.roll(v, 7, 0)
                )
                best = pick(pick(v, ring[r]), ring[r + 2])
                best = pick(best, pick(below, above))
                best = pick(best, pick(pltpu.roll(v, 1, 1), pltpu.roll(v, 127, 1)))
                bounds[f, r, 2 + at] = best

    def outer_part(n, t, f):
        target = lax.rem(t + 1, 3)
        _, rest = shares(t)
        for r in range(ROWS):
            x = [
                [[partial[f, i, j, k, r] for k in range(3)] for j in range(3)] for i in range(3)
            ]
            up_y, down_y = [rest * coef[12 + 8 * r + n] for n in range(2)]
            for k in range(3):
                for j in range(3):
                    if r == 0:
                        up_x = rest * coef[22]
                        x[0][j][k] = x[0][j][k] + up_x * recv_x[n, 0, 3 * j + k]
                    if r == ROWS - 1:
                        down_x = rest * coef[23 + 2 * ROWS]
                        x[2][j][k] = x[2][j][k] - down_x * recv_x[n, 1, 3 * j + k]
                for i in range(3):
                    at = 9 * r + 3 * i + k
                    x[i][0][k] = x[i][0][k] + up_y * spread(recv_y[n, 0, at : at + 1, :])
                    x[i][2][k] = x[i][2][k] - down_y * spread(recv_y[n, 1, at : at + 1, :])
            averages, tops, bottoms = [], [], []
            for i in range(3):
                for j in range(3):
                    lo, mid, hi = x[i][j]
                    tops.append(jnp.maximum(jnp.maximum(lo, hi), mid))
                    bottoms.append(jnp.minimum(jnp.minimum(lo, hi), mid))
                    line = (lo + hi) + 4.0 * mid
                    weight = NODE_WEIGHTS[i] * NODE_WEIGHTS[j]
                    averages.append(line if weight == 1.0 else weight * line)
            average = tree(jnp.add, averages) * (1.0 / 216.0)
            largest = tree(jnp.maximum, tops)
            smallest = tree(jnp.minimum, bottoms)
            lowest = bounds[f, r, 2]
            highest = bounds[f, r, 3]
            upper = (jnp.maximum(highest - average, 0.0) + SOFTNESS) / (largest - average + SOFTNESS)
            lower = (jnp.maximum(average - lowest, 0.0) + SOFTNESS) / (average - smallest + SOFTNESS)
            scaling = jnp.minimum(1.0, jnp.minimum(upper, lower))
            offset = average - scaling * average
            for i in range(3):
                for j in range(3):
                    for k in range(3):
                        x[i][j][k] = scaling * x[i][j][k] + offset
                        state[target, f, i, j, k, r] = x[i][j][k]
            pack_faces(n + FIELDS, r, x)
            pack_bounds(n + FIELDS, f, r, scaling * smallest + offset, scaling * largest + offset)

    def stage(n, _):
        t = lax.div(n, FIELDS)
        f = n - FIELDS * t
        part = lax.rem(t, 3)

        @pl.when(t == 0)
        def _():
            begin(f)

        wait_faces(n, part, face_recv_sem)

        @pl.when(part == 0)
        def _():
            gather_bounds(n, f)

        outer_part(n, t, f)

        @pl.when(t < STAGES - 1)
        def _():
            start_faces(n + FIELDS, lax.rem(part + 1, 3))
            inner_part(t + 1, f)

        wait_faces(n, part, face_send_sem)

        @pl.when(t == STAGES - 1)
        def _():
            out[f] = state[0, f]

        return 0

    speed_y.wait_send()
    speed_x.wait_send()
    for phase, received in enumerate((near_max, far_max)):
        n = received.shape[0]
        if n > 1:
            pltpu.make_async_copy(
                received.at[pl.ds(1, n - 1)], received.at[pl.ds(1, n - 1)], max_send_sem.at[phase]
            ).wait()

    lax.fori_loop(0, STAGES * FIELDS, stage, 0)


def solution(mesh):
    n_slab, n_sub = mesh.shape["slab"], mesh.shape["sub"]
    n_near = 16
    n_far = n_slab * n_sub // n_near

    def on_device(fields, speeds):
        vmem = lambda *shape: pltpu.VMEM(shape, jnp.float32)
        dma = lambda *shape: pltpu.SemaphoreType.DMA(shape)
        return pl.pallas_call(
            functools.partial(kernel, n_slab, n_sub),
            out_shape=pltpu.VMEM(fields.shape, fields.dtype),
            in_specs=[pl.BlockSpec(memory_space=pltpu.HBM)] * 2,
            out_specs=pl.BlockSpec(memory_space=pltpu.VMEM),
            scratch_shapes=[
                vmem(3, FIELDS, 3, 3, 3, ROWS, 8, 128),
                vmem(FIELDS, 3, 3, 3, ROWS, 8, 128),
                vmem(3, ROWS, 8, 128),
                vmem(FIELDS, ROWS, 4, 8, 128),
                vmem(24 + 2 * ROWS, 8, 128),
                vmem((STAGES + 1) * FIELDS, 2, X_TILES, 8, 128),
                vmem(STAGES * FIELDS, 2, X_TILES, 8, 128),
                vmem((STAGES + 1) * FIELDS, 2, Y_ROWS, 128),
                vmem(STAGES * FIELDS, 2, Y_ROWS, 128),
                vmem(8, 128),
                vmem(8, 128),
                vmem(8, 128),
                vmem(n_near, 1, 128),
                vmem(n_far, 1, 128),
                vmem(2, 1, 128),
                vmem(2 * (Y_USED + 8 * X_TILES) + 4, 128),
                dma(2),
                dma(2 * FIELDS),
                dma(2 * FIELDS),
                dma(2),
                dma(2),
                dma(2),
                dma(2),
            ],
            compiler_params=pltpu.CompilerParams(
                collective_id=1, has_side_effects=True, vmem_limit_bytes=60 * 1024 * 1024
            ),
            name="remap",
        )(fields, speeds)

    spec = P(None, None, None, None, "slab", "sub", None)
    return jax.shard_map(
        on_device,
        mesh=mesh,
        in_specs=(spec, P(None, "slab", "sub", None)),
        out_specs=spec,
        check_vma=False,
    )
```

```python
import functools

import jax
import jax.numpy as jnp
from jax import lax
from jax.experimental import pallas as pl
from jax.experimental.pallas import tpu as pltpu
from jax.sharding import PartitionSpec as P

STEPS = 3
STAGES = 3 * STEPS
FIELDS = 3
ROWS = 2
COURANT = 0.12
SOFTNESS = 0.05
NODE_WEIGHTS = (1.0, 4.0, 1.0)
MESH = pl.DeviceIdType.MESH
X_TILES, X_NODES = 11, 9
Y_ROWS, Y_USED, Y_NODES = 24, 22, 18


def tree(pick, values):
    while len(values) > 1:
        values = [
            pick(values[n], values[n + 1]) if n + 1 < len(values) else values[n]
            for n in range(0, len(values), 2)
        ]
    return values[0]


def line_terms(v0, v1, v2, a, flux_lo, flux_hi):
    d = v2 - v0
    t = (v0 + v2) + 4.0 * v1
    big = a * t
    small = a * d
    twice = small + small
    return (big - twice) + flux_lo, small, -((big + twice) + flux_hi)


def kernel(
    n_slab,
    n_sub,
    fields_hbm,
    speeds_hbm,
    out,
    state,
    partial,
    speeds,
    bounds,
    coef,
    send_x,
    recv_x,
    send_y,
    recv_y,
    speed_send,
    speed_recv_x,
    speed_recv_y,
    near_max,
    far_max,
    max_send,
    measure,
    load_sem,
    face_send_sem,
    face_recv_sem,
    speed_send_sem,
    speed_recv_sem,
    max_send_sem,
    max_recv_sem,
):
    slab = lax.axis_index("slab")
    sub = lax.axis_index("sub")
    n_z, n_x = n_slab // 8, n_sub // 2

    def shifted(at, by, size):
        moved = at + by
        return jnp.where(moved >= size, moved - size, moved)

    z, l = lax.div(slab, 8), lax.rem(slab, 8)
    x, h = lax.div(sub, 2), lax.rem(sub, 2)
    n_near, n_far = near_max.shape[0], far_max.shape[0]

    def near_device(by):
        at = shifted(8 * h + l, by, n_near)
        half = jnp.where(at >= 8, 1, 0)
        return {"slab": 8 * z + at - 8 * half, "sub": 2 * x + half}

    def far_device(by):
        at = shifted(n_x * z + x, by, n_far)
        plane = lax.div(at, n_x)
        return {"slab": 8 * plane + l, "sub": 2 * (at - n_x * plane) + h}

    def for_partners(n, action):
        def body(step, _):
            away = lax.div(step + 1, 2)
            action(n // 2 + jnp.where(lax.rem(step, 2) == 1, -away, away))
            return 0

        lax.fori_loop(0, n - 1, body, 0)

    neighbours = []
    for axis, at, size, odd in (("sub", sub, n_sub, h), ("slab", slab, n_slab, lax.rem(l, 2))):
        after = shifted(at, 1, size)
        before = shifted(at, size - 1, size)
        neighbours.append((axis, 1 - odd, {axis: jnp.where(odd == 1, after, before)}))
        neighbours.append((axis, odd, {axis: jnp.where(odd == 1, before, after)}))
    previous = {"sub": {"sub": shifted(sub, n_sub - 1, n_sub)}, "slab": {"slab": shifted(slab, n_slab - 1, n_slab)}}


    barrier = pltpu.get_barrier_semaphore()
    def greet(device):
        pl.semaphore_signal(barrier, inc=1, device_id=device, device_id_type=MESH)

    for _, _, device in neighbours:
        greet(device)
    load_speeds = pltpu.make_async_copy(speeds_hbm, speeds, load_sem.at[0])
    load_speeds.start()
    load_fields = pltpu.make_async_copy(fields_hbm, state.at[0], load_sem.at[1])
    load_fields.start()
    for_partners(n_far, lambda by: greet(far_device(by)))
    for_partners(n_near, lambda by: greet(near_device(by)))
    load_speeds.wait()
    for r in range(ROWS):
        speed_send[r : r + 1, :] = speeds[1, r, 0:1, :]
    pl.semaphore_wait(barrier, len(neighbours) + (n_far - 1) + (n_near - 1))

    speed_y = pltpu.make_async_remote_copy(
        src_ref=speed_send,
        dst_ref=speed_recv_y,
        send_sem=speed_send_sem.at[0],
        recv_sem=speed_recv_sem.at[0],
        device_id=previous["sub"],
        device_id_type=MESH,
    )
    speed_x = pltpu.make_async_remote_copy(
        src_ref=speeds.at[0, 0],
        dst_ref=speed_recv_x,
        send_sem=speed_send_sem.at[1],
        recv_sem=speed_recv_sem.at[1],
        device_id=previous["slab"],
        device_id_type=MESH,
    )
    speed_y.start()
    speed_x.start()

    def face_copies(n, with_bounds, axes=("sub", "slab")):
        copies = []
        for axis, way, device in neighbours:
            if axis not in axes:
                continue
            if axis == "sub":
                sent, received, size = send_y, recv_y, Y_USED if with_bounds else Y_NODES
            else:
                sent, received, size = send_x, recv_x, X_TILES if with_bounds else X_NODES
            copies.append(
                pltpu.make_async_remote_copy(
                    src_ref=sent.at[n, way, pl.ds(0, size)],
                    dst_ref=received.at[n, way, pl.ds(0, size)],
                    send_sem=face_send_sem.at[lax.rem(n, 2 * FIELDS)],
                    recv_sem=face_recv_sem.at[lax.rem(n, 2 * FIELDS)],
                    device_id=device,
                    device_id_type=MESH,
                )
            )
        return copies

    def start_faces(n, part, axes):
        @pl.when(part == 0)
        def _():
            for copy in face_copies(n, True, axes):
                copy.start()

        @pl.when(part != 0)
        def _():
            for copy in face_copies(n, False, axes):
                copy.start()

    def wait_rows(rows, sem):
        pltpu.make_async_copy(measure.at[pl.ds(0, rows)], measure.at[pl.ds(0, rows)], sem).wait()

    def wait_faces(n, part, sems):
        @pl.when(part == 0)
        def _():
            wait_rows(2 * (Y_USED + 8 * X_TILES), sems.at[lax.rem(n, 2 * FIELDS)])

        @pl.when(part != 0)
        def _():
            wait_rows(2 * (Y_NODES + 8 * X_NODES), sems.at[lax.rem(n, 2 * FIELDS)])

    def pack_sub(n, r, values):
        for i in range(3):
            for k in range(3):
                at = 9 * r + 3 * i + k
                send_y[n, 0, at : at + 1, :] = values[i][2][k][7:8, :]
                send_y[n, 1, at : at + 1, :] = values[i][0][k][0:1, :]

    def pack_slab(n, r, values):
        for j in range(3):
            for k in range(3):
                if r == ROWS - 1:
                    send_x[n, 0, 3 * j + k] = values[2][j][k]
                if r == 0:
                    send_x[n, 1, 3 * j + k] = values[0][j][k]

    def pack_bounds(n, f, r, lowest, highest):
        for which, v in ((0, lowest), (1, highest)):
            bounds[f, r, which] = v
            if r == ROWS - 1:
                send_x[n, 0, 9 + which] = v
            if r == 0:
                send_x[n, 1, 9 + which] = v
            at = 18 + 2 * r + which
            send_y[n, 0, at : at + 1, :] = v[7:8, :]
            send_y[n, 1, at : at + 1, :] = v[0:1, :]

    def first_faces(f, _):
        for r in range(ROWS):
            values = [
                [[state[0, f, i, j, k, r] for k in range(3)] for j in range(3)] for i in range(3)
            ]
            flat = [values[i][j][k] for i in range(3) for j in range(3) for k in range(3)]
            pack_sub(f, r, values)
            pack_slab(f, r, values)
            pack_bounds(
                f, f, r, tree(jnp.minimum, flat), tree(jnp.maximum, flat)
            )
        return 0

    def send_first(f, _):
        for copy in face_copies(f, True):
            copy.start()
        return 0

    load_fields.wait()
    lax.fori_loop(0, FIELDS, first_faces, 0)

    row_at = lax.broadcasted_iota(jnp.int32, (8, 128), 0)
    at_bottom = row_at == 0
    at_top = row_at == 7

    speed_y.wait_recv()
    speed_x.wait_recv()
    face_x = [speeds[0, r] for r in range(ROWS)] + [speed_recv_x[...]]
    y_lo = [speeds[1, r] for r in range(ROWS)]
    y_hi = [
        jnp.where(
            at_top,
            jnp.broadcast_to(speed_recv_y[r : r + 1, :], (8, 128)),
            pltpu.roll(y_lo[r], 7, 0),
        )
        for r in range(ROWS)
    ]
    z_lo = [speeds[2, r] for r in range(ROWS)]
    interiors = [
        [0.5 * (face_x[r] + face_x[r + 1]) for r in range(ROWS)],
        [0.5 * (y_lo[r] + y_hi[r]) for r in range(ROWS)],
        [0.5 * (z_lo[r] + pltpu.roll(z_lo[r], 127, 1)) for r in range(ROWS)],
    ]
    fast = None
    for r in range(ROWS):
        total = jnp.abs(interiors[0][r]) + jnp.abs(interiors[1][r]) + jnp.abs(interiors[2][r])
        fast = total if fast is None else jnp.maximum(fast, total)
    fast = jnp.max(fast, axis=0, keepdims=True)
    def coefficients():
        up = lambda s: 6.0 * jnp.maximum(s, 0.0)
        down = lambda s: 6.0 * jnp.minimum(s, 0.0)
        tiles = [-interiors[d][r] for r in range(ROWS) for d in range(3)]
        for r in range(ROWS):
            y_up, y_down = up(y_lo[r]), down(y_hi[r])
            tiles += [
                jnp.where(at_bottom, 0.0, y_up),
                down(y_lo[r]),
                up(y_hi[r]),
                jnp.where(at_top, 0.0, y_down),
                up(z_lo[r]),
                down(z_lo[r]),
                jnp.where(at_bottom, y_up, 0.0),
                jnp.where(at_top, y_down, 0.0),
            ]
        for q in range(ROWS + 1):
            tiles += [up(face_x[q]), down(face_x[q])]
        return tiles

    def shares(t):
        part = lax.rem(t, 3)
        pick = lambda *values: jnp.where(
            part == 0, values[0], jnp.where(part == 1, values[1], values[2])
        ).astype(jnp.float32)
        return pick(0.0, 0.75, 1.0 / 3.0), pick(1.0, 0.25, 2.0 / 3.0)

    def inner_part(t, f, rate_only=False):
        source = lax.rem(t, 3)
        share, rest = shares(t)
        for r in range(ROWS):
            v = [
                [[state[source, f, i, j, k, r] for k in range(3)] for j in range(3)]
                for i in range(3)
            ]
            new = [
                [[None if rate_only else v[i][j][k] for k in range(3)] for j in range(3)]
                for i in range(3)
            ]
            a = [coef[3 * r + d] for d in range(3)]
            up_x = [coef[22 + 2 * q] for q in (r, r + 1)]
            down_x = [coef[23 + 2 * q] for q in (r, r + 1)]
            up_y, down_y, up_y_hi, down_y_hi, up_z, down_z = [coef[6 + 8 * r + n] for n in range(6)]
            for k in range(3):
                for j in range(3):
                    flux_lo = down_x[0] * v[0][j][k]
                    if r > 0:
                        flux_lo = flux_lo + up_x[0] * state[source, f, 2, j, k, r - 1]
                    flux_hi = up_x[1] * v[2][j][k]
                    if r < ROWS - 1:
                        flux_hi = flux_hi + down_x[1] * state[source, f, 0, j, k, r + 1]
                    terms = line_terms(v[0][j][k], v[1][j][k], v[2][j][k], a[0], flux_lo, flux_hi)
                    for i in range(3):
                        new[i][j][k] = terms[i] if rate_only else new[i][j][k] + terms[i]
                for i in range(3):
                    flux_lo = up_y * pltpu.roll(v[i][2][k], 1, 0) + down_y * v[i][0][k]
                    flux_hi = up_y_hi * v[i][2][k] + down_y_hi * pltpu.roll(v[i][0][k], 7, 0)
                    terms = line_terms(v[i][0][k], v[i][1][k], v[i][2][k], a[1], flux_lo, flux_hi)
                    for j in range(3):
                        new[i][j][k] = new[i][j][k] + terms[j]
            for i in range(3):
                for j in range(3):
                    flux_lo = up_z * pltpu.roll(v[i][j][2], 1, 1) + down_z * v[i][j][0]
                    flux_hi = pltpu.roll(flux_lo, 127, 1)
                    terms = line_terms(v[i][j][0], v[i][j][1], v[i][j][2], a[2], flux_lo, flux_hi)
                    for k in range(3):
                        x = new[i][j][k] + terms[k]
                        if not rate_only:
                            x = share * state[0, f, i, j, k, r] + rest * x
                        partial[f, i, j, k, r] = x

    for phase, (received, device_of) in enumerate(((near_max, near_device), (far_max, far_device))):
        n = received.shape[0]
        received[0] = fast
        if n > 1:
            max_send[phase] = fast

            def send(by):
                pltpu.make_async_remote_copy(
                    src_ref=max_send.at[phase],
                    dst_ref=received.at[by],
                    send_sem=max_send_sem.at[phase],
                    recv_sem=max_recv_sem.at[phase],
                    device_id=device_of(by),
                    device_id_type=MESH,
                ).start()

            for_partners(n, send)
            if phase == 0:
                lax.fori_loop(0, FIELDS, send_first, 0)
                for at, v in enumerate(coefficients()):
                    coef[at] = v
                lax.fori_loop(0, FIELDS, lambda f, _: (inner_part(0, f, True), 0)[1], 0)
            pltpu.make_async_copy(
                received.at[pl.ds(1, n - 1)], received.at[pl.ds(1, n - 1)], max_recv_sem.at[phase]
            ).wait()
            fast = jnp.max(received[...], axis=0)
    fastest = jnp.max(jnp.broadcast_to(fast, (8, 128)), axis=1, keepdims=True)
    time_step = COURANT / (jnp.broadcast_to(fastest, (8, 128)) + 1e-6)
    for at in range(coef.shape[0]):
        coef[at] = time_step * coef[at]

    def begin(f):
        for r in range(ROWS):
            for i in range(3):
                for j in range(3):
                    for k in range(3):
                        at = (f, i, j, k, r)
                        partial[at] = state[(0, *at)] + time_step * partial[at]

    def spread(row):
        return jnp.broadcast_to(row, (8, 128))

    def gather_bounds(n, f):
        for at, pick in ((0, jnp.minimum), (1, jnp.maximum)):
            values = [bounds[f, r, at] for r in range(ROWS)]
            ring = [recv_x[n, 0, 9 + at]] + values + [recv_x[n, 1, 9 + at]]
            for r in range(ROWS):
                here = 18 + 2 * r + at
                v = values[r]
                below = jnp.where(
                    at_bottom, spread(recv_y[n, 0, here : here + 1, :]), pltpu.roll(v, 1, 0)
                )
                above = jnp.where(
                    at_top, spread(recv_y[n, 1, here : here + 1, :]), pltpu.roll(v, 7, 0)
                )
                best = pick(pick(v, ring[r]), ring[r + 2])
                best = pick(best, pick(below, above))
                best = pick(best, pick(pltpu.roll(v, 1, 1), pltpu.roll(v, 127, 1)))
                bounds[f, r, 2 + at] = best

    def outer_part(n, t, f):
        target = lax.rem(t + 1, 3)
        _, rest = shares(t)
        limited = []
        for r in range(ROWS):
            x = [
                [[partial[f, i, j, k, r] for k in range(3)] for j in range(3)] for i in range(3)
            ]
            up_y, down_y = [rest * coef[12 + 8 * r + n] for n in range(2)]
            for k in range(3):
                for j in range(3):
                    if r == 0:
                        up_x = rest * coef[22]
                        x[0][j][k] = x[0][j][k] + up_x * recv_x[n, 0, 3 * j + k]
                    if r == ROWS - 1:
                        down_x = rest * coef[23 + 2 * ROWS]
                        x[2][j][k] = x[2][j][k] - down_x * recv_x[n, 1, 3 * j + k]
                for i in range(3):
                    at = 9 * r + 3 * i + k
                    x[i][0][k] = x[i][0][k] + up_y * spread(recv_y[n, 0, at : at + 1, :])
                    x[i][2][k] = x[i][2][k] - down_y * spread(recv_y[n, 1, at : at + 1, :])
            averages, tops, bottoms = [], [], []
            for i in range(3):
                for j in range(3):
                    lo, mid, hi = x[i][j]
                    tops.append(jnp.maximum(jnp.maximum(lo, hi), mid))
                    bottoms.append(jnp.minimum(jnp.minimum(lo, hi), mid))
                    line = (lo + hi) + 4.0 * mid
                    weight = NODE_WEIGHTS[i] * NODE_WEIGHTS[j]
                    averages.append(line if weight == 1.0 else weight * line)
            average = tree(jnp.add, averages) * (1.0 / 216.0)
            largest = tree(jnp.maximum, tops)
            smallest = tree(jnp.minimum, bottoms)
            lowest = bounds[f, r, 2]
            highest = bounds[f, r, 3]
            upper = (jnp.maximum(highest - average, 0.0) + SOFTNESS) / (largest - average + SOFTNESS)
            lower = (jnp.maximum(average - lowest, 0.0) + SOFTNESS) / (average - smallest + SOFTNESS)
            scaling = jnp.minimum(1.0, jnp.minimum(upper, lower))
            offset = average - scaling * average
            for i in range(3):
                for j in range(3):
                    for k in range(3):
                        x[i][j][k] = scaling * x[i][j][k] + offset
            pack_sub(n + FIELDS, r, x)
            pack_bounds(n + FIELDS, f, r, scaling * smallest + offset, scaling * largest + offset)
            limited.append(x)

        @pl.when(t < STAGES - 1)
        def _():
            start_faces(n + FIELDS, lax.rem(t + 1, 3), ("sub",))

        for r in range(ROWS):
            pack_slab(n + FIELDS, r, limited[r])
            for i in range(3):
                for j in range(3):
                    for k in range(3):
                        state[target, f, i, j, k, r] = limited[r][i][j][k]

    def stage(n, _):
        t = lax.div(n, FIELDS)
        f = n - FIELDS * t
        part = lax.rem(t, 3)

        @pl.when(t == 0)
        def _():
            begin(f)

        wait_faces(n, part, face_recv_sem)

        @pl.when(part == 0)
        def _():
            gather_bounds(n, f)

        outer_part(n, t, f)

        @pl.when(t < STAGES - 1)
        def _():
            start_faces(n + FIELDS, lax.rem(part + 1, 3), ("slab",))
            inner_part(t + 1, f)

        wait_faces(n, part, face_send_sem)

        @pl.when(t == STAGES - 1)
        def _():
            out[f] = state[0, f]

        return 0

    speed_y.wait_send()
    speed_x.wait_send()
    for phase, received in enumerate((near_max, far_max)):
        n = received.shape[0]
        if n > 1:
            pltpu.make_async_copy(
                received.at[pl.ds(1, n - 1)], received.at[pl.ds(1, n - 1)], max_send_sem.at[phase]
            ).wait()

    lax.fori_loop(0, STAGES * FIELDS, stage, 0)


def solution(mesh):
    n_slab, n_sub = mesh.shape["slab"], mesh.shape["sub"]
    n_near = 16
    n_far = n_slab * n_sub // n_near

    def on_device(fields, speeds):
        vmem = lambda *shape: pltpu.VMEM(shape, jnp.float32)
        dma = lambda *shape: pltpu.SemaphoreType.DMA(shape)
        return pl.pallas_call(
            functools.partial(kernel, n_slab, n_sub),
            out_shape=pltpu.VMEM(fields.shape, fields.dtype),
            in_specs=[pl.BlockSpec(memory_space=pltpu.HBM)] * 2,
            out_specs=pl.BlockSpec(memory_space=pltpu.VMEM),
            scratch_shapes=[
                vmem(3, FIELDS, 3, 3, 3, ROWS, 8, 128),
                vmem(FIELDS, 3, 3, 3, ROWS, 8, 128),
                vmem(3, ROWS, 8, 128),
                vmem(FIELDS, ROWS, 4, 8, 128),
                vmem(24 + 2 * ROWS, 8, 128),
                vmem((STAGES + 1) * FIELDS, 2, X_TILES, 8, 128),
                vmem(STAGES * FIELDS, 2, X_TILES, 8, 128),
                vmem((STAGES + 1) * FIELDS, 2, Y_ROWS, 128),
                vmem(STAGES * FIELDS, 2, Y_ROWS, 128),
                vmem(8, 128),
                vmem(8, 128),
                vmem(8, 128),
                vmem(n_near, 1, 128),
                vmem(n_far, 1, 128),
                vmem(2, 1, 128),
                vmem(2 * (Y_USED + 8 * X_TILES) + 4, 128),
                dma(2),
                dma(2 * FIELDS),
                dma(2 * FIELDS),
                dma(2),
                dma(2),
                dma(2),
                dma(2),
            ],
            compiler_params=pltpu.CompilerParams(
                collective_id=1, has_side_effects=True, vmem_limit_bytes=60 * 1024 * 1024
            ),
            name="remap",
        )(fields, speeds)

    spec = P(None, None, None, None, "slab", "sub", None)
    return jax.shard_map(
        on_device,
        mesh=mesh,
        in_specs=(spec, P(None, "slab", "sub", None)),
        out_specs=spec,
        check_vma=False,
    )
```
